512 devices in a mesh: grid: 128 (over z, y, core), band: 4 (over x).
Axes of the slice: x: 4, y: 4, z: 16, core: 2. Of those that a mesh axis runs over, the one named last changes fastest.
Arguments:
- orbitals: bfloat16 [1024, 131072], P(('grid', 'band')), may hold values from -6 to 128
- pivots: int32 [1024], replicated, may hold values from 0 to 131071, as said below
Outputs:
- localized: bfloat16 [1024, 131072], P(('grid', 'band'))
The draws below stay inside these ranges and needn't reach their ends.
Inputs may be any that keep to these rules, and one draw needn't show every extreme that they name: Distinct grid points. Pivot j belongs to block (j // 2) % 4; in every block at most 8 pivots lie in one slab of 1024 consecutive grid points, and in every block some slab holds exactly 8 of them.
All inputs are finite; a program needn't handle non-finite values.
Results may differ from the reference program's by a relative error of at most 0.0044.
The reference program's roundings to bfloat16 on the way (of `pivot_rows`, `products` and `inverse`) count: a program that leaves them out, or rounds other values in their place, can miss the bound.
Values may be sent and summed in bfloat16 or wider, within the bound.
A program may use at most 128 MiB of HBM per device.

```python
import math
import jax
import jax.numpy as jnp
from jax import lax

NB = 1024
G_DEV = 1024
NG = 131072
JB = 256
PER = 2
MOST = 8
N_GRID = 128
N_BAND = 4


def pivot_table(key):
    table = jax.vmap(lambda slab_key: jax.random.permutation(slab_key, G_DEV))(jax.random.split(jax.random.fold_in(key, 101), N_GRID))
    blocks = []
    for block in range(N_BAND):
        block_key = jax.random.fold_in(key, 200 + block)
        first_key, second_key, third_key = jax.random.split(block_key, 3)
        forced = jax.random.randint(first_key, (), 0, N_GRID).astype(jnp.int32)
        chosen = jax.random.permutation(second_key, (N_GRID - 1) * MOST)[:JB - MOST].astype(jnp.int32)
        others = chosen // MOST
        others = others + (others >= forced).astype(jnp.int32)
        owners = jnp.concatenate([jnp.full((MOST,), forced, jnp.int32), others])
        ranks = jnp.concatenate([jnp.arange(MOST, dtype=jnp.int32), chosen % MOST])
        shuffle = jax.random.permutation(third_key, JB)
        owners = owners[shuffle]
        ranks = ranks[shuffle]
        points = owners * G_DEV + table[owners, block * MOST + ranks].astype(jnp.int32)
        blocks.append(points.astype(jnp.int32))
    stacked = jnp.stack(blocks, 0).reshape(N_BAND, N_GRID, PER)
    return stacked.transpose(1, 0, 2).reshape(NB).astype(jnp.int32)


def draw_pivots(key, part):
    common = pivot_table(key)
    return common


def draw_orbitals(key, part):
    common = pivot_table(key)
    key = jax.random.fold_in(key, 7)
    values = jnp.clip(jax.random.normal(key, (NB, NG), jnp.float32), -6.0, 6.0)
    values = values.at[jnp.arange(NB), common].set(NB / 8.0)
    return values.astype(jnp.bfloat16)


def setup_inputs(seed: int = 0) -> dict:
    key_list = jax.random.split(jax.random.key(seed), 3)
    orbitals = draw_orbitals(jax.random.fold_in(key_list[2], 71), 0)
    pivots = draw_pivots(jax.random.fold_in(key_list[2], 71), 0)
    return {"orbitals": orbitals, "pivots": pivots}


def reference(orbitals, pivots):
    wide = orbitals.astype(jnp.float32)
    pivot_rows = jnp.take(wide, pivots, axis=1).T
    products = (jnp.dot(pivot_rows.astype(jnp.float32), wide.astype(jnp.float32), preferred_element_type=jnp.float32, precision=lax.Precision.HIGHEST) * (1.0 / math.sqrt(NB))).astype(jnp.bfloat16)
    narrow = products.astype(jnp.float32)
    gram = jnp.dot(narrow.astype(jnp.float32), narrow.T.astype(jnp.float32), preferred_element_type=jnp.float32, precision=lax.Precision.HIGHEST) / NG
    factor = jnp.linalg.cholesky(gram)
    identity = jnp.eye(NB, dtype=jnp.float32)
    inverse = lax.linalg.triangular_solve(factor, identity, left_side=True, lower=True).astype(jnp.bfloat16)
    return jnp.dot(inverse.astype(jnp.float32), narrow.astype(jnp.float32), preferred_element_type=jnp.float32, precision=lax.Precision.HIGHEST).astype(jnp.bfloat16)
```

```python
import functools
import math

import jax
import jax.numpy as jnp
from jax import lax
from jax.experimental import pallas as pl
from jax.experimental.pallas import tpu as pltpu
from jax.sharding import PartitionSpec as P

MESH = pl.DeviceIdType.MESH
X, Y, Z, CORES = 4, 4, 16, 2
NB = 1024
BLOCK = 128
BLOCKS = NB // BLOCK
TILES = 576
OWNERS = 9
ROWS_OF_CORE = ((0, 3, 4, 7), (1, 2, 5, 6))
VMEM = 56 * 1024 * 1024


def place():
    grid = lax.axis_index("grid")
    return lax.axis_index("band"), lax.rem(grid // CORES, Y), grid // (CORES * Y), lax.rem(grid, CORES)


def device(x, y, z, core):
    return ((z * Y + y) * CORES + core, x)


def greet(x, y, z, core, plane):
    barrier = pltpu.get_barrier_semaphore()
    partners = [device(x, y, z, 1 - core)]
    for along_y in range(Y):
        for along_x in range(X):
            if (along_x or along_y) and (plane or not (along_x and along_y)):
                partners.append(device(lax.rem(x + along_x, X), lax.rem(y + along_y, Y), z, core))
    for step in range(1, Z):
        partners.append(device(x, y, lax.rem(z + step, Z), core))
    for partner in partners:
        pl.semaphore_signal(barrier, inc=1, device_id=partner, device_id_type=MESH)
    pl.semaphore_wait(barrier, len(partners))


def remote(src, dst, send, recv, target):
    return pltpu.make_async_remote_copy(
        src_ref=src, dst_ref=dst, send_sem=send, recv_sem=recv, device_id=target, device_id_type=MESH
    )


def spread(out, unit, x, y, z, core, send, recv):
    half = 16 * unit
    base = core * 2 * half
    firsts = (x, y)
    seconds = (y, x)

    def mate(axis_is_x, step):
        if axis_is_x:
            return device(lax.rem(x + step, X), y, z, core)
        return device(x, lax.rem(y + step, Y), z, core)

    started = []
    inner = []
    for h in range(2):
        mine = out.at[pl.ds(base + h * half + (firsts[h] * 4 + seconds[h]) * unit, unit)]
        for step in range(1, 4):
            copy = remote(mine, mine, send.at[0, h, step], recv.at[0, h, step], mate(h == 1, step))
            copy.start()
            inner.append(copy)
    for copy in inner:
        copy.wait_recv()
    started += inner
    sibling = device(x, y, z, 1 - core)
    across = []
    near = []
    block = 4 * unit

    def part(h, where, begin=0, size=block):
        return out.at[pl.ds(base + h * half + lax.rem(firsts[h] + where, 4) * block + begin, size)]

    def forward(h, index, ref):
        copy = remote(ref, ref, send.at[2, h, index], recv.at[2, h, index], sibling)
        copy.start()
        across.append(copy)

    for h in range(2):
        for index, step in ((0, 1), (1, 3)):
            copy = remote(part(h, 0), part(h, 0), send.at[1, h, index], recv.at[1, h, index], mate(h == 0, step))
            copy.start()
            near.append((h, index, step, copy))
    for h in range(2):
        forward(h, 0, part(h, 0))
    far = []
    for h, index, step, copy in near:
        copy.wait_recv()
        ref = part(h, 4 - step, index * (block // 2), block // 2)
        onward = remote(ref, ref, send.at[1, h, 2 + index], recv.at[1, h, 2 + index], mate(h == 0, step))
        onward.start()
        far.append(onward)
        forward(h, 1 + index, part(h, 4 - step))
        started.append(copy)
    for copy in far:
        copy.wait_recv()
    for h in range(2):
        forward(h, 3, part(h, 2))
    for copy in across:
        copy.wait_recv()
    for copy in started + far + across:
        copy.wait_send()


def order_of_z():
    steps = []
    for step in range(1, Z // 2 + 1):
        steps.append(step)
        if step != Z - step:
            steps.append(Z - step)
    return steps


class Regroup:
    def __init__(self, source, out, beside, landed, sems, spot):
        self.source, self.out, self.beside, self.landed = source, out, beside, landed
        self.p_send, self.p_recv, self.z_send, self.z_recv, self.y_send, self.y_recv, self.local = sems
        self.x, self.y, self.z, self.core = spot
        self.origin = (self.core, 1 - self.core)
        self.pair = remote(
            source.at[:, :, 1 - self.core], beside, self.p_send, self.p_recv,
            device(self.x, self.y, self.z, 1 - self.core),
        )
        self.done = []
        self.paths = []
        self.plane = []

    def leaving(self, path, z):
        return self.source.at[z, :, self.core] if path == 0 else self.beside.at[z]

    def start_z(self, path):
        x, y, z, core = self.x, self.y, self.z, self.core
        if path == 1:
            self.pair.wait_recv()
        landing = self.landed.at[self.origin[path], z]
        copies = []
        for step in order_of_z():
            target = lax.rem(z + step, Z)
            copy = remote(
                self.leaving(path, target), landing, self.z_send.at[path, step], self.z_recv.at[path, step],
                device(x, y, target, core),
            )
            copy.start()
            copies.append(copy)
        own = pltpu.make_async_copy(self.leaving(path, z), landing, self.local.at[path])
        own.start()
        self.paths.append((own, copies))

    def start_plane(self, path):
        x, y, z, core = self.x, self.y, self.z, self.core
        own, copies = self.paths[path]
        own.wait()
        for copy in copies:
            copy.wait_recv()
        self.done += copies
        origin = self.origin[path]
        landing = self.out.at[:, y, origin, x]
        for along_y in range(Y):
            for along_x in range(X):
                if along_x or along_y:
                    to_x, to_y = lax.rem(x + along_x, X), lax.rem(y + along_y, Y)
                    index = along_y * X + along_x
                    copy = remote(
                        self.landed.at[origin, :, to_y, to_x], landing,
                        self.y_send.at[path, index], self.y_recv.at[path, index],
                        device(to_x, to_y, z, core),
                    )
                    copy.start()
                    self.plane.append(copy)
        keep = pltpu.make_async_copy(self.landed.at[origin, :, y, x], landing, self.local.at[2 + path])
        keep.start()
        self.done_keep = getattr(self, "done_keep", []) + [keep]

    def finish(self):
        for copy in self.plane:
            copy.wait_recv()
        for keep in self.done_keep:
            keep.wait()
        for copy in self.plane + self.done + [self.pair]:
            copy.wait_send()


def regroup_scratch(points):
    return [
        pltpu.VMEM((Z, Y, X, 2, points), jnp.bfloat16),
        pltpu.VMEM((CORES, Z, Y, X, 2, points), jnp.bfloat16),
        pltpu.SemaphoreType.DMA,
        pltpu.SemaphoreType.DMA,
        pltpu.SemaphoreType.DMA((2, Z)),
        pltpu.SemaphoreType.DMA((2, Z)),
        pltpu.SemaphoreType.DMA((2, X * Y)),
        pltpu.SemaphoreType.DMA((2, X * Y)),
        pltpu.SemaphoreType.DMA((4,)),
    ]


def gather_kernel(orbitals, piece, slab, rows, beside, landed, *sems):
    moving, sems = sems[:7], sems[7:]
    q_send, q_recv, send, recv = sems
    x, y, z, core = place()
    greet(x, y, z, core, True)
    regroup = Regroup(orbitals, slab, beside, landed, moving, (x, y, z, core))
    regroup.pair.start()
    first = []
    for step in order_of_z():
        copy = remote(
            piece, rows.at[z, y, core, x], q_send.at[step], q_recv.at[step], device(x, y, lax.rem(z + step, Z), core)
        )
        copy.start()
        first.append(copy)
    regroup.start_z(0)
    regroup.start_z(1)
    rows[z, y, core, x] = piece[...]
    for copy in first:
        copy.wait_recv()
    second = []
    mine = rows.at[:, y, core, x]
    for step in range(1, Y):
        copy = remote(
            mine, mine, send.at[0, step], recv.at[0, step], device(x, lax.rem(y + step, Y), z, core)
        )
        copy.start()
        second.append(copy)
    for copy in second:
        copy.wait_recv()
    sibling = device(x, y, z, 1 - core)
    near, far, last = [], [], []

    def along_x(step):
        return device(lax.rem(x + step, X), y, z, core)

    def forward(index, ref):
        copy = remote(ref, ref, send.at[2, index], recv.at[2, index], sibling)
        copy.start()
        last.append(copy)

    mine = rows.at[:, :, core, x]
    for index, step in ((0, 1), (1, 3)):
        copy = remote(mine, mine, send.at[1, index], recv.at[1, index], along_x(step))
        copy.start()
        near.append(copy)
    forward(0, mine)
    for index, step in ((0, 1), (1, 3)):
        near[index].wait_recv()
        source = lax.rem(x + 4 - step, X)
        ref = rows.at[pl.ds(index * (Z // 2), Z // 2), :, core, source]
        copy = remote(ref, ref, send.at[1, 2 + index], recv.at[1, 2 + index], along_x(step))
        copy.start()
        far.append(copy)
        forward(1 + index, rows.at[:, :, core, source])
    regroup.start_plane(0)
    for copy in far:
        copy.wait_recv()
    forward(3, rows.at[:, :, core, lax.rem(x + 2, X)])
    regroup.start_plane(1)
    for copy in last:
        copy.wait_recv()
    regroup.finish()
    for copy in first + second + near + far + last:
        copy.wait_send()


def gather(orbitals, piece):
    points = orbitals.shape[-1]
    return pl.pallas_call(
        gather_kernel,
        out_shape=[
            jax.ShapeDtypeStruct((Z, Y, CORES, X, 2, points), jnp.bfloat16),
            jax.ShapeDtypeStruct((Z, Y, CORES, X, 16, 128), jnp.bfloat16),
        ],
        in_specs=[pl.BlockSpec(memory_space=pltpu.VMEM)] * 2,
        out_specs=[pl.BlockSpec(memory_space=pltpu.VMEM)] * 2,
        scratch_shapes=regroup_scratch(points) + [
            pltpu.SemaphoreType.DMA((Z,)),
            pltpu.SemaphoreType.DMA((Z,)),
            pltpu.SemaphoreType.DMA((3, 4)),
            pltpu.SemaphoreType.DMA((3, 4)),
        ],
        compiler_params=pltpu.CompilerParams(
            collective_id=0, has_side_effects=True, vmem_limit_bytes=32 * 1024 * 1024
        ),
        name="gather_slab_and_pivot_rows",
    )(orbitals, piece)


def return_kernel(local, out, beside, landed, *sems):
    x, y, z, core = place()
    greet(x, y, z, core, True)
    regroup = Regroup(local, out, beside, landed, sems, (x, y, z, core))
    regroup.pair.start()
    regroup.start_z(0)
    regroup.start_z(1)
    regroup.start_plane(0)
    regroup.start_plane(1)
    regroup.finish()


def give_back(local):
    points = local.shape[-1]
    return pl.pallas_call(
        return_kernel,
        out_shape=jax.ShapeDtypeStruct(local.shape, jnp.bfloat16),
        in_specs=[pl.BlockSpec(memory_space=pltpu.VMEM)],
        out_specs=pl.BlockSpec(memory_space=pltpu.VMEM),
        scratch_shapes=regroup_scratch(points),
        compiler_params=pltpu.CompilerParams(
            collective_id=2, has_side_effects=True, vmem_limit_bytes=32 * 1024 * 1024
        ),
        name="return_localized",
    )(local)


def gram_kernel(products, out, theirs, terms, got0, got1, got2, got3, send, recv, r_send, r_recv, z_send, z_recv, g_send, g_recv, p_send, p_recv):
    x, y, z, core = place()
    greet(x, y, z, core, False)
    pair = remote(products, theirs, p_send, p_recv, device(x, y, z, 1 - core))
    pair.start()
    pair.wait_recv()
    contract = (((1,), (1,)), ((), ()))

    for which in range(CORES):

        @pl.when(core == which)
        def _():
            count = 0
            for i in ROWS_OF_CORE[which]:
                rows = slice(i * BLOCK, (i + 1) * BLOCK)
                rest = slice(i * BLOCK, NB)
                row = lax.dot_general(
                    products[rows, :], products[rest, :], contract, preferred_element_type=jnp.float32
                ) + lax.dot_general(
                    theirs[rows, :], theirs[rest, :], contract, preferred_element_type=jnp.float32
                )
                for j in range(BLOCKS - i):
                    terms[count * 16:(count + 1) * 16] = row[:, j * BLOCK:(j + 1) * BLOCK].reshape(16, 8, 128)
                    count += 1

    unit = OWNERS
    half = 16 * unit
    firsts = (x, y)
    seconds = (y, x)

    def mate(axis_is_x, step):
        if axis_is_x:
            return device(lax.rem(x + step, X), y, z, core)
        return device(x, lax.rem(y + step, Y), z, core)

    block = 4 * unit
    middle = block // 2

    def span(h, where, begin=0, size=block):
        return pl.ds(h * half + lax.rem(firsts[h] + where, 4) * block + begin, size)

    copies = []
    for h in range(2):
        for index, step in ((0, 1), (1, 3)):
            copy = remote(
                terms.at[span(h, 2, index * middle, middle)], got0.at[h, index],
                r_send.at[0, h, index], r_recv.at[0, h, index], mate(h == 0, step),
            )
            copy.start()
            copies.append((h, index, step, copy))
    near = []
    for h, index, step, copy in copies:
        copy.wait_recv()
        part = span(h, step, index * middle, middle)
        terms[part] = terms[part] + got0[h, index]
        onward = remote(
            terms.at[span(h, step)], got1.at[h, index], r_send.at[2, h, index], r_recv.at[2, h, index],
            mate(h == 0, step),
        )
        onward.start()
        near.append(onward)
    copies = [copy for _, _, _, copy in copies] + near
    for copy in near:
        copy.wait_recv()
    for h in range(2):
        mine = span(h, 0)
        terms[mine] = terms[mine] + (got1[h, 0] + got1[h, 1])
    later = []
    for step in range(1, 4):
        for h in range(2):
            target = lax.rem(seconds[h] + step, 4)
            copy = remote(
                terms.at[pl.ds(h * half + (firsts[h] * 4 + target) * unit, unit)],
                got2.at[h, step - 1],
                r_send.at[1, h, step],
                r_recv.at[1, h, step],
                mate(h == 1, step),
            )
            copy.start()
            later.append(copy)
    for copy in later:
        copy.wait_recv()
    starts = [h * half + (firsts[h] * 4 + seconds[h]) * unit for h in range(2)]
    for h in range(2):
        mine = pl.ds(starts[h], unit)
        terms[mine] = terms[mine] + (got2[h, 0] + got2[h, 1]) + got2[h, 2]

    def to_owner(step, h):
        target = lax.rem(z + step, Z)
        tile = jnp.minimum(target, OWNERS - 1)
        return target, remote(
            terms.at[starts[h] + tile],
            got3.at[step - 1, h],
            z_send.at[step, h],
            z_recv.at[step, h],
            device(x, y, target, core),
        )

    for step in range(1, Z):
        for h in range(2):
            target, copy = to_owner(step, h)

            @pl.when(target < OWNERS)
            def _():
                copy.start()

    goals = [core * 2 * half + starts[h] for h in range(2)]
    tile = jnp.minimum(z, OWNERS - 1)

    def to_all(step, h):
        return remote(
            out.at[goals[h] + tile],
            out.at[goals[h] + tile],
            g_send.at[step, h],
            g_recv.at[step, h],
            device(x, y, lax.rem(z + step, Z), core),
        )

    @pl.when(z < OWNERS)
    def _():
        for step in range(1, Z):
            for h in range(2):
                to_owner(step, h)[1].wait_recv()
        for h in range(2):
            total = terms[starts[h] + tile]
            for step in range(1, Z):
                total = total + got3[step - 1, h]
            out[goals[h] + tile] = total
        for step in range(1, Z):
            for h in range(2):
                to_all(step, h).start()

    for step in range(1, Z):
        source = lax.rem(z + Z - step, Z)

        @pl.when(source < OWNERS)
        def _():
            for h in range(2):
                to_all(step, h).wait_recv()

    spread(out, unit, x, y, z, core, send, recv)

    for step in range(1, Z):
        for h in range(2):
            target, copy = to_owner(step, h)

            @pl.when(target < OWNERS)
            def _():
                copy.wait_send()

    @pl.when(z < OWNERS)
    def _():
        for step in range(1, Z):
            for h in range(2):
                to_all(step, h).wait_send()

    for copy in copies + later:
        copy.wait_send()
    pair.wait_send()


def sum_gram(products):
    unit = OWNERS
    return pl.pallas_call(
        gram_kernel,
        out_shape=jax.ShapeDtypeStruct((TILES, 8, 128), jnp.float32),
        in_specs=[pl.BlockSpec(memory_space=pltpu.VMEM)],
        out_specs=pl.BlockSpec(memory_space=pltpu.VMEM),
        scratch_shapes=[
            pltpu.VMEM(products.shape, jnp.bfloat16),
            pltpu.VMEM((TILES // 2, 8, 128), jnp.float32),
            pltpu.VMEM((2, 2, 2 * unit, 8, 128), jnp.float32),
            pltpu.VMEM((2, 2, 4 * unit, 8, 128), jnp.float32),
            pltpu.VMEM((2, 3, unit, 8, 128), jnp.float32),
            pltpu.VMEM((Z - 1, 2, 8, 128), jnp.float32),
            pltpu.SemaphoreType.DMA((3, 2, 4)),
            pltpu.SemaphoreType.DMA((3, 2, 4)),
            pltpu.SemaphoreType.DMA((3, 2, 4)),
            pltpu.SemaphoreType.DMA((3, 2, 4)),
            pltpu.SemaphoreType.DMA((Z, 2)),
            pltpu.SemaphoreType.DMA((Z, 2)),
            pltpu.SemaphoreType.DMA((Z, 2)),
            pltpu.SemaphoreType.DMA((Z, 2)),
            pltpu.SemaphoreType.DMA,
            pltpu.SemaphoreType.DMA,
        ],
        compiler_params=pltpu.CompilerParams(
            collective_id=1, has_side_effects=True, vmem_limit_bytes=32 * 1024 * 1024
        ),
        name="sum_gram",
    )(products)


def split(value):
    high = value.astype(jnp.bfloat16)
    return high, (value - high.astype(jnp.float32)).astype(jnp.bfloat16)


def dot(a, b):
    return jnp.dot(a, b, preferred_element_type=jnp.float32)


def factor_block(load, lane, row):
    full = (8, 128)
    groups = [load(g) for g in range(16)]
    for quarter in range(4):
        first = 4 * quarter
        for g in range(first, first + 4):
            at = 8 * g
            panel = groups[g]
            columns = [jnp.broadcast_to(panel[:, at + t:at + t + 1], full) for t in range(8)]
            a = [[jnp.broadcast_to(columns[t][i:i + 1, :], full) for t in range(i + 1)] for i in range(8)]
            below = [[None] * 8 for _ in range(8)]
            scale = []
            for s in range(8):
                r = lax.rsqrt(a[s][s])
                scale.append(r)
                for i in range(s + 1, 8):
                    below[i][s] = a[i][s] * r
                for i in range(s + 1, 8):
                    for t in range(s + 1, i + 1):
                        a[i][t] = a[i][t] - below[i][s] * below[t][s]
            inside = (lane >= at) & (lane < at + 8)
            panel = jnp.where(inside, (lane == row + at).astype(jnp.float32), panel)
            solved = []
            for s in range(8):
                value = jnp.broadcast_to(panel[s:s + 1, :], full)
                for t in range(s):
                    value = value - below[s][t] * solved[t]
                solved.append(value * scale[s])
            result = solved[0]
            for s in range(1, 8):
                result = jnp.where(row == s, solved[s], result)
            groups[g] = result
            for other in range(g + 1, first + 4):
                target = groups[other]
                left = []
                for s in range(8):
                    value = jnp.broadcast_to(target[:, at + s:at + s + 1], full)
                    for t in range(s):
                        value = value - below[s][t] * left[t]
                    left.append(value * scale[s])
                target = jnp.where(inside, 0.0, target)
                for s in range(8):
                    target = target - left[s] * solved[s]
                groups[other] = target
        if quarter < 3:
            at = 32 * quarter
            inside = (lane >= at) & (lane < at + 32)
            rows = jnp.concatenate(
                [
                    jnp.where(inside & (lane > 8 * g + row), 0.0, groups[g])
                    for g in range(first, first + 4)
                ],
                axis=0,
            )
            turned = rows.T[at + 32:, :]
            high, low = split(rows)
            turned_high, turned_low = split(turned)
            change = dot(turned_high, high) + dot(turned_low, high) + dot(turned_high, low)
            for other in range(first + 4, 16):
                begin = (other - first - 4) * 8
                groups[other] = jnp.where(inside, 0.0, groups[other]) - change[begin:begin + 8, :]
    return [jnp.where(lane > 8 * g + row, 0.0, groups[g]) for g in range(16)]


def solve_kernel(gram, products, out, mat, inverse):
    lane = lax.broadcasted_iota(jnp.int32, (8, 128), 1)
    row = lax.broadcasted_iota(jnp.int32, (8, 128), 0)
    count = 0
    for rows in ROWS_OF_CORE:
        for i in rows:
            for j in range(i, BLOCKS):
                mat[i * BLOCK:(i + 1) * BLOCK, j * BLOCK:(j + 1) * BLOCK] = (
                    gram[count * 16:(count + 1) * 16].reshape(BLOCK, BLOCK) / 131072.0
                )
                count += 1
            if i:
                mat[i * BLOCK:(i + 1) * BLOCK, :i * BLOCK] = jnp.zeros((BLOCK, i * BLOCK), jnp.float32)

    def step(k, carry):
        begin = pl.multiple_of(k * BLOCK, BLOCK)
        own = pl.ds(begin, BLOCK)

        def load(g):
            return mat[pl.ds(pl.multiple_of(begin + 8 * g, 8), 8), own]

        for g, value in enumerate(factor_block(load, lane, row)):
            mat[pl.ds(pl.multiple_of(begin + 8 * g, 8), 8), own] = value
        for kk in range(BLOCKS):

            @pl.when(k == kk)
            def _():
                at = kk * BLOCK
                high, low = split(mat[at:at + BLOCK, at:at + BLOCK])
                left = jnp.concatenate([high, low], axis=1)
                spans = [(0, at), (at + BLOCK, NB)]
                for start, stop in spans:
                    if start < stop:
                        up, down = split(mat[at:at + BLOCK, start:stop])
                        mat[at:at + BLOCK, start:stop] = dot(left, jnp.concatenate([up, up], axis=0)) + dot(high, down)
                if kk + 1 < BLOCKS:
                    after = at + BLOCK
                    turned_high, turned_low = split(mat[at:at + BLOCK, after:].T)
                    turned = jnp.concatenate([turned_high, turned_low], axis=1)
                    for start in range(0, NB, 256):
                        up, down = split(mat[at:at + BLOCK, start:start + 256])
                        change = dot(turned, jnp.concatenate([up, up], axis=0)) + dot(turned_high, down)
                        if start <= at < start + 256:
                            for part in (start, start + BLOCK):
                                piece = change[:, part - start:part - start + BLOCK]
                                if part == at:
                                    mat[after:, part:part + BLOCK] = -piece
                                else:
                                    mat[after:, part:part + BLOCK] = mat[after:, part:part + BLOCK] - piece
                        else:
                            mat[after:, start:start + 256] = mat[after:, start:start + 256] - change

        return carry

    lax.fori_loop(0, BLOCKS, step, 0)
    for i in range(BLOCKS):
        at = i * BLOCK
        inverse[at:at + BLOCK, :at + BLOCK] = mat[at:at + BLOCK, :at + BLOCK].astype(jnp.bfloat16)
    for i in range(BLOCKS):
        at = i * BLOCK
        out[at:at + BLOCK, :] = dot(
            inverse[at:at + BLOCK, :at + BLOCK], products[:at + BLOCK, :]
        ).astype(jnp.bfloat16)


def solve(gram, products):
    return pl.pallas_call(
        solve_kernel,
        out_shape=jax.ShapeDtypeStruct(products.shape, jnp.bfloat16),
        in_specs=[pl.BlockSpec(memory_space=pltpu.VMEM)] * 2,
        out_specs=pl.BlockSpec(memory_space=pltpu.VMEM),
        scratch_shapes=[pltpu.VMEM((NB, NB), jnp.float32), pltpu.VMEM((NB, NB), jnp.bfloat16)],
        compiler_params=pltpu.CompilerParams(vmem_limit_bytes=VMEM),
        name="factor_and_localize",
    )(gram, products)


def pick(orbitals, pivots):
    folded = orbitals.reshape(2, 1024, 128)
    outer = (pivots[:, None] // 128 == jnp.arange(1024, dtype=jnp.int32)[None, :]).astype(jnp.bfloat16)
    inner = pivots[:, None] % 128 == jnp.arange(128, dtype=jnp.int32)[None, :]
    rows = jnp.einsum("jh,rhl->rjl", outer, folded, preferred_element_type=jnp.float32)
    return jnp.sum(jnp.where(inner[None], rows, 0.0), axis=2).astype(jnp.bfloat16)


def body(orbitals, pivots):
    points = orbitals.shape[1] // 512
    entries = (Z, Y, CORES, X, 2, points)
    piece = pick(orbitals, pivots).reshape(16, 128)
    outgoing = orbitals.reshape(2, 512, points).transpose(1, 0, 2).reshape(entries)
    slab, rows = gather(outgoing, piece)
    products = (
        lax.dot_general(
            rows.reshape(NB, NB), slab.reshape(NB, points), (((0,), (0,)), ((), ())),
            preferred_element_type=jnp.float32,
        )
        * (1.0 / math.sqrt(NB))
    ).astype(jnp.bfloat16)
    gram = sum_gram(products)
    local = solve(gram, products)
    returned = give_back(local.reshape(entries))
    return returned.reshape(512, 2, points).transpose(1, 0, 2).reshape(orbitals.shape)


def solution(mesh):
    placed = (P(("grid", "band"), None), P())
    return jax.shard_map(
        body, mesh=mesh, in_specs=placed, out_specs=P(("grid", "band"), None), check_vma=False
    )
```

```python
import functools
import math

import jax
import jax.numpy as jnp
from jax import lax
from jax.experimental import pallas as pl
from jax.experimental.pallas import tpu as pltpu
from jax.sharding import PartitionSpec as P

MESH = pl.DeviceIdType.MESH
X, Y, Z, CORES = 4, 4, 16, 2
NB = 1024
BLOCK = 128
BLOCKS = NB // BLOCK
TILES = 576
OWNERS = 9
ROWS_OF_CORE = ((0, 3, 4, 7), (1, 2, 5, 6))
VMEM = 56 * 1024 * 1024


def place():
    grid = lax.axis_index("grid")
    return lax.axis_index("band"), lax.rem(grid // CORES, Y), grid // (CORES * Y), lax.rem(grid, CORES)


def device(x, y, z, core):
    return ((z * Y + y) * CORES + core, x)


def greet(x, y, z, core, plane):
    barrier = pltpu.get_barrier_semaphore()
    partners = [device(x, y, z, 1 - core)]
    for along_y in range(Y):
        for along_x in range(X):
            if (along_x or along_y) and (plane or not (along_x and along_y)):
                partners.append(device(lax.rem(x + along_x, X), lax.rem(y + along_y, Y), z, core))
    for step in range(1, Z):
        partners.append(device(x, y, lax.rem(z + step, Z), core))
    for partner in partners:
        pl.semaphore_signal(barrier, inc=1, device_id=partner, device_id_type=MESH)
    pl.semaphore_wait(barrier, len(partners))


def remote(src, dst, send, recv, target):
    return pltpu.make_async_remote_copy(
        src_ref=src, dst_ref=dst, send_sem=send, recv_sem=recv, device_id=target, device_id_type=MESH
    )


def spread(out, unit, x, y, z, core, send, recv):
    half = 16 * unit
    base = core * 2 * half
    firsts = (x, y)
    seconds = (y, x)

    def mate(axis_is_x, step):
        if axis_is_x:
            return device(lax.rem(x + step, X), y, z, core)
        return device(x, lax.rem(y + step, Y), z, core)

    started = []
    inner = []
    for h in range(2):
        mine = out.at[pl.ds(base + h * half + (firsts[h] * 4 + seconds[h]) * unit, unit)]
        for step in range(1, 4):
            copy = remote(mine, mine, send.at[0, h, step], recv.at[0, h, step], mate(h == 1, step))
            copy.start()
            inner.append(copy)
    for copy in inner:
        copy.wait_recv()
    started += inner
    sibling = device(x, y, z, 1 - core)
    across = []
    near = []
    block = 4 * unit

    def part(h, where, begin=0, size=block):
        return out.at[pl.ds(base + h * half + lax.rem(firsts[h] + where, 4) * block + begin, size)]

    def forward(h, index, ref):
        copy = remote(ref, ref, send.at[2, h, index], recv.at[2, h, index], sibling)
        copy.start()
        across.append(copy)

    for h in range(2):
        for index, step in ((0, 1), (1, 3)):
            copy = remote(part(h, 0), part(h, 0), send.at[1, h, index], recv.at[1, h, index], mate(h == 0, step))
            copy.start()
            near.append((h, index, step, copy))
    for h in range(2):
        forward(h, 0, part(h, 0))
    far = []
    for h, index, step, copy in near:
        copy.wait_recv()
        ref = part(h, 4 - step, index * (block // 2), block // 2)
        onward = remote(ref, ref, send.at[1, h, 2 + index], recv.at[1, h, 2 + index], mate(h == 0, step))
        onward.start()
        far.append(onward)
        forward(h, 1 + index, part(h, 4 - step))
        started.append(copy)
    for copy in far:
        copy.wait_recv()
    for h in range(2):
        forward(h, 3, part(h, 2))
    for copy in across:
        copy.wait_recv()
    for copy in started + far + across:
        copy.wait_send()


def order_of_z():
    steps = []
    for step in range(1, Z // 2 + 1):
        steps.append(step)
        if step != Z - step:
            steps.append(Z - step)
    return steps


class Regroup:
    def __init__(self, source, out, beside, landed, sems, spot):
        self.source, self.out, self.beside, self.landed = source, out, beside, landed
        self.p_send, self.p_recv, self.z_send, self.z_recv, self.y_send, self.y_recv, self.local = sems
        self.x, self.y, self.z, self.core = spot
        self.origin = (self.core, 1 - self.core)
        self.pair = remote(
            source.at[:, :, 1 - self.core], beside, self.p_send, self.p_recv,
            device(self.x, self.y, self.z, 1 - self.core),
        )
        self.done = []
        self.paths = []
        self.plane = []

    def leaving(self, path, z):
        return self.source.at[z, :, self.core] if path == 0 else self.beside.at[z]

    def start_z(self, path):
        x, y, z, core = self.x, self.y, self.z, self.core
        if path == 1:
            self.pair.wait_recv()
        landing = self.landed.at[self.origin[path], z]
        copies = []
        for step in order_of_z():
            target = lax.rem(z + step, Z)
            copy = remote(
                self.leaving(path, target), landing, self.z_send.at[path, step], self.z_recv.at[path, step],
                device(x, y, target, core),
            )
            copy.start()
            copies.append(copy)
        own = pltpu.make_async_copy(self.leaving(path, z), landing, self.local.at[path])
        own.start()
        self.paths.append((own, copies))

    def start_plane(self, path):
        x, y, z, core = self.x, self.y, self.z, self.core
        own, copies = self.paths[path]
        own.wait()
        for copy in copies:
            copy.wait_recv()
        self.done += copies
        origin = self.origin[path]
        landing = self.out.at[:, y, origin, x]
        for along_y in range(Y):
            for along_x in range(X):
                if along_x or along_y:
                    to_x, to_y = lax.rem(x + along_x, X), lax.rem(y + along_y, Y)
                    index = along_y * X + along_x
                    copy = remote(
                        self.landed.at[origin, :, to_y, to_x], landing,
                        self.y_send.at[path, index], self.y_recv.at[path, index],
                        device(to_x, to_y, z, core),
                    )
                    copy.start()
                    self.plane.append(copy)
        keep = pltpu.make_async_copy(self.landed.at[origin, :, y, x], landing, self.local.at[2 + path])
        keep.start()
        self.done_keep = getattr(self, "done_keep", []) + [keep]

    def finish(self):
        for copy in self.plane:
            copy.wait_recv()
        for keep in self.done_keep:
            keep.wait()
        for copy in self.plane + self.done + [self.pair]:
            copy.wait_send()


def regroup_scratch(points):
    return [
        pltpu.VMEM((Z, Y, X, 2, points), jnp.bfloat16),
        pltpu.VMEM((CORES, Z, Y, X, 2, points), jnp.bfloat16),
        pltpu.SemaphoreType.DMA,
        pltpu.SemaphoreType.DMA,
        pltpu.SemaphoreType.DMA((2, Z)),
        pltpu.SemaphoreType.DMA((2, Z)),
        pltpu.SemaphoreType.DMA((2, X * Y)),
        pltpu.SemaphoreType.DMA((2, X * Y)),
        pltpu.SemaphoreType.DMA((4,)),
    ]


def gather_kernel(orbitals, piece, slab, rows, beside, landed, *sems):
    moving, sems = sems[:7], sems[7:]
    q_send, q_recv, send, recv = sems
    x, y, z, core = place()
    greet(x, y, z, core, True)
    regroup = Regroup(orbitals, slab, beside, landed, moving, (x, y, z, core))
    regroup.pair.start()
    first = []
    for step in order_of_z():
        copy = remote(
            piece, rows.at[z, y, core, x], q_send.at[step], q_recv.at[step], device(x, y, lax.rem(z + step, Z), core)
        )
        copy.start()
        first.append(copy)
    regroup.start_z(0)
    regroup.start_z(1)
    rows[z, y, core, x] = piece[...]
    for copy in first:
        copy.wait_recv()
    second = []
    mine = rows.at[:, y, core, x]
    for step in range(1, Y):
        copy = remote(
            mine, mine, send.at[0, step], recv.at[0, step], device(x, lax.rem(y + step, Y), z, core)
        )
        copy.start()
        second.append(copy)
    for copy in second:
        copy.wait_recv()
    sibling = device(x, y, z, 1 - core)
    near, far, last = [], [], []

    def along_x(step):
        return device(lax.rem(x + step, X), y, z, core)

    def forward(index, ref):
        copy = remote(ref, ref, send.at[2, index], recv.at[2, index], sibling)
        copy.start()
        last.append(copy)

    mine = rows.at[:, :, core, x]
    for index, step in ((0, 1), (1, 3)):
        copy = remote(mine, mine, send.at[1, index], recv.at[1, index], along_x(step))
        copy.start()
        near.append(copy)
    forward(0, mine)
    for index, step in ((0, 1), (1, 3)):
        near[index].wait_recv()
        source = lax.rem(x + 4 - step, X)
        ref = rows.at[pl.ds(index * (Z // 2), Z // 2), :, core, source]
        copy = remote(ref, ref, send.at[1, 2 + index], recv.at[1, 2 + index], along_x(step))
        copy.start()
        far.append(copy)
        forward(1 + index, rows.at[:, :, core, source])
    regroup.start_plane(0)
    for copy in far:
        copy.wait_recv()
    forward(3, rows.at[:, :, core, lax.rem(x + 2, X)])
    regroup.start_plane(1)
    for copy in last:
        copy.wait_recv()
    regroup.finish()
    for copy in first + second + near + far + last:
        copy.wait_send()


def gather(orbitals, piece):
    points = orbitals.shape[-1]
    return pl.pallas_call(
        gather_kernel,
        out_shape=[
            jax.ShapeDtypeStruct((Z, Y, CORES, X, 2, points), jnp.bfloat16),
            jax.ShapeDtypeStruct((Z, Y, CORES, X, 16, 128), jnp.bfloat16),
        ],
        in_specs=[pl.BlockSpec(memory_space=pltpu.VMEM)] * 2,
        out_specs=[pl.BlockSpec(memory_space=pltpu.VMEM)] * 2,
        scratch_shapes=regroup_scratch(points) + [
            pltpu.SemaphoreType.DMA((Z,)),
            pltpu.SemaphoreType.DMA((Z,)),
            pltpu.SemaphoreType.DMA((3, 4)),
            pltpu.SemaphoreType.DMA((3, 4)),
        ],
        compiler_params=pltpu.CompilerParams(
            collective_id=0, has_side_effects=True, vmem_limit_bytes=32 * 1024 * 1024
        ),
        name="gather_slab_and_pivot_rows",
    )(orbitals, piece)


def return_kernel(landed, out, send, recv, kept):
    x, y, z, core = place()
    barrier = pltpu.get_barrier_semaphore()
    partners = []
    for along_y in range(Y):
        for along_x in range(X):
            if along_x or along_y:
                partners.append((lax.rem(x + along_x, X), lax.rem(y + along_y, Y), along_y * X + along_x))
    for to_x, to_y, _ in partners:
        pl.semaphore_signal(barrier, inc=1, device_id=device(to_x, to_y, z, core), device_id_type=MESH)
    pl.semaphore_wait(barrier, len(partners))
    landing = out.at[:, y, :, x]
    copies = []
    for to_x, to_y, index in partners:
        copy = remote(
            landed.at[:, :, to_y, to_x], landing, send.at[index], recv.at[index], device(to_x, to_y, z, core)
        )
        copy.start()
        copies.append(copy)
    keep = pltpu.make_async_copy(landed.at[:, :, y, x], landing, kept)
    keep.start()
    keep.wait()
    for copy in copies:
        copy.wait_recv()
    for copy in copies:
        copy.wait_send()


def give_back(landed):
    points = landed.shape[-1]
    dma = pltpu.SemaphoreType.DMA
    return pl.pallas_call(
        return_kernel,
        out_shape=jax.ShapeDtypeStruct((Z, Y, CORES, X, 2, points), jnp.bfloat16),
        in_specs=[pl.BlockSpec(memory_space=pltpu.VMEM)],
        out_specs=pl.BlockSpec(memory_space=pltpu.VMEM),
        scratch_shapes=[dma((X * Y,)), dma((X * Y,)), dma],
        compiler_params=pltpu.CompilerParams(
            collective_id=2, has_side_effects=True, vmem_limit_bytes=16 * 1024 * 1024
        ),
        name="return_localized",
    )(landed)


def gram_kernel(products, landed, out, theirs, terms, got0, got1, got2, got3, mat, ready, beside, send, recv, r_send, r_recv, z_send, z_recv, g_send, g_recv, p_send, p_recv, *leave):
    x, y, z, core = place()
    greet(x, y, z, core, False)
    pair = remote(products, theirs, p_send, p_recv, device(x, y, z, 1 - core))
    pair.start()
    pair.wait_recv()
    contract = (((1,), (1,)), ((), ()))

    for which in range(CORES):

        @pl.when(core == which)
        def _():
            count = 0
            for i in ROWS_OF_CORE[which]:
                rows = slice(i * BLOCK, (i + 1) * BLOCK)
                rest = slice(i * BLOCK, NB)
                row = lax.dot_general(
                    products[rows, :], products[rest, :], contract, preferred_element_type=jnp.float32
                ) + lax.dot_general(
                    theirs[rows, :], theirs[rest, :], contract, preferred_element_type=jnp.float32
                )
                for j in range(BLOCKS - i):
                    terms[count * 16:(count + 1) * 16] = row[:, j * BLOCK:(j + 1) * BLOCK].reshape(16, 8, 128)
                    count += 1

    unit = OWNERS
    half = 16 * unit
    firsts = (x, y)
    seconds = (y, x)

    def mate(axis_is_x, step):
        if axis_is_x:
            return device(lax.rem(x + step, X), y, z, core)
        return device(x, lax.rem(y + step, Y), z, core)

    block = 4 * unit
    middle = block // 2

    def span(h, where, begin=0, size=block):
        return pl.ds(h * half + lax.rem(firsts[h] + where, 4) * block + begin, size)

    copies = []
    for h in range(2):
        for index, step in ((0, 1), (1, 3)):
            copy = remote(
                terms.at[span(h, 2, index * middle, middle)], got0.at[h, index],
                r_send.at[0, h, index], r_recv.at[0, h, index], mate(h == 0, step),
            )
            copy.start()
            copies.append((h, index, step, copy))
    near = []
    for h, index, step, copy in copies:
        copy.wait_recv()
        part = span(h, step, index * middle, middle)
        terms[part] = terms[part] + got0[h, index]
        onward = remote(
            terms.at[span(h, step)], got1.at[h, index], r_send.at[2, h, index], r_recv.at[2, h, index],
            mate(h == 0, step),
        )
        onward.start()
        near.append(onward)
    copies = [copy for _, _, _, copy in copies] + near
    for copy in near:
        copy.wait_recv()
    for h in range(2):
        mine = span(h, 0)
        terms[mine] = terms[mine] + (got1[h, 0] + got1[h, 1])
    later = []
    for step in range(1, 4):
        for h in range(2):
            target = lax.rem(seconds[h] + step, 4)
            copy = remote(
                terms.at[pl.ds(h * half + (firsts[h] * 4 + target) * unit, unit)],
                got2.at[h, step - 1],
                r_send.at[1, h, step],
                r_recv.at[1, h, step],
                mate(h == 1, step),
            )
            copy.start()
            later.append(copy)
    for copy in later:
        copy.wait_recv()
    starts = [h * half + (firsts[h] * 4 + seconds[h]) * unit for h in range(2)]
    for h in range(2):
        mine = pl.ds(starts[h], unit)
        terms[mine] = terms[mine] + (got2[h, 0] + got2[h, 1]) + got2[h, 2]

    def to_owner(step, h):
        target = lax.rem(z + step, Z)
        tile = jnp.minimum(target, OWNERS - 1)
        return target, remote(
            terms.at[starts[h] + tile],
            got3.at[step - 1, h],
            z_send.at[step, h],
            z_recv.at[step, h],
            device(x, y, target, core),
        )

    for step in range(1, Z):
        for h in range(2):
            target, copy = to_owner(step, h)

            @pl.when(target < OWNERS)
            def _():
                copy.start()

    goals = [core * 2 * half + starts[h] for h in range(2)]
    tile = jnp.minimum(z, OWNERS - 1)

    def to_all(step, h):
        return remote(
            out.at[goals[h] + tile],
            out.at[goals[h] + tile],
            g_send.at[step, h],
            g_recv.at[step, h],
            device(x, y, lax.rem(z + step, Z), core),
        )

    @pl.when(z < OWNERS)
    def _():
        for step in range(1, Z):
            for h in range(2):
                to_owner(step, h)[1].wait_recv()
        for h in range(2):
            total = terms[starts[h] + tile]
            for step in range(1, Z):
                total = total + got3[step - 1, h]
            out[goals[h] + tile] = total
        for step in range(1, Z):
            for h in range(2):
                to_all(step, h).start()

    for step in range(1, Z):
        source = lax.rem(z + Z - step, Z)

        @pl.when(source < OWNERS)
        def _():
            for h in range(2):
                to_all(step, h).wait_recv()

    spread(out, unit, x, y, z, core, send, recv)

    for step in range(1, Z):
        for h in range(2):
            target, copy = to_owner(step, h)

            @pl.when(target < OWNERS)
            def _():
                copy.wait_send()

    @pl.when(z < OWNERS)
    def _():
        for step in range(1, Z):
            for h in range(2):
                to_all(step, h).wait_send()

    for copy in copies + later:
        copy.wait_send()
    pair.wait_send()
    solve(out, products, landed, mat, ready, beside, leave, (x, y, z, core))


def localize(products):
    unit = OWNERS
    points = products.shape[1]
    dma = pltpu.SemaphoreType.DMA
    return pl.pallas_call(
        gram_kernel,
        out_shape=jax.ShapeDtypeStruct((Z, CORES, Y * X * 2, points), jnp.bfloat16),
        in_specs=[pl.BlockSpec(memory_space=pltpu.VMEM)],
        out_specs=pl.BlockSpec(memory_space=pltpu.VMEM),
        scratch_shapes=[
            pltpu.VMEM((TILES, 8, 128), jnp.float32),
            pltpu.VMEM(products.shape, jnp.bfloat16),
            pltpu.VMEM((TILES // 2, 8, 128), jnp.float32),
            pltpu.VMEM((2, 2, 2 * unit, 8, 128), jnp.float32),
            pltpu.VMEM((2, 2, 4 * unit, 8, 128), jnp.float32),
            pltpu.VMEM((2, 3, unit, 8, 128), jnp.float32),
            pltpu.VMEM((Z - 1, 2, 8, 128), jnp.float32),
            pltpu.VMEM((NB, NB), jnp.float32),
            pltpu.VMEM((BLOCKS, CORES, 2, Y * X * 2, points), jnp.bfloat16),
            pltpu.VMEM((BLOCKS, 2, Y * X * 2, points), jnp.bfloat16),
            dma((3, 2, 4)),
            dma((3, 2, 4)),
            dma((3, 2, 4)),
            dma((3, 2, 4)),
            dma((Z, 2)),
            dma((Z, 2)),
            dma((Z, 2)),
            dma((Z, 2)),
            dma,
            dma,
            dma((BLOCKS,)),
            dma((BLOCKS,)),
            dma((2, Z)),
            dma((2, Z)),
            dma((2,)),
        ],
        compiler_params=pltpu.CompilerParams(collective_id=1, has_side_effects=True, vmem_limit_bytes=VMEM),
        name="sum_factor_and_localize",
    )(products)


def split(value):
    high = value.astype(jnp.bfloat16)
    return high, (value - high.astype(jnp.float32)).astype(jnp.bfloat16)


def dot(a, b):
    return jnp.dot(a, b, preferred_element_type=jnp.float32)


def factor_block(load, lane, row):
    full = (8, 128)
    groups = [load(g) for g in range(16)]
    for quarter in range(4):
        first = 4 * quarter
        for g in range(first, first + 4):
            at = 8 * g
            panel = groups[g]
            columns = [jnp.broadcast_to(panel[:, at + t:at + t + 1], full) for t in range(8)]
            a = [[jnp.broadcast_to(columns[t][i:i + 1, :], full) for t in range(i + 1)] for i in range(8)]
            below = [[None] * 8 for _ in range(8)]
            scale = []
            for s in range(8):
                r = lax.rsqrt(a[s][s])
                scale.append(r)
                for i in range(s + 1, 8):
                    below[i][s] = a[i][s] * r
                for i in range(s + 1, 8):
                    for t in range(s + 1, i + 1):
                        a[i][t] = a[i][t] - below[i][s] * below[t][s]
            inside = (lane >= at) & (lane < at + 8)
            panel = jnp.where(inside, (lane == row + at).astype(jnp.float32), panel)
            solved = []
            for s in range(8):
                value = jnp.broadcast_to(panel[s:s + 1, :], full)
                for t in range(s):
                    value = value - below[s][t] * solved[t]
                solved.append(value * scale[s])
            result = solved[0]
            for s in range(1, 8):
                result = jnp.where(row == s, solved[s], result)
            groups[g] = result
            for other in range(g + 1, first + 4):
                target = groups[other]
                left = []
                for s in range(8):
                    value = jnp.broadcast_to(target[:, at + s:at + s + 1], full)
                    for t in range(s):
                        value = value - below[s][t] * left[t]
                    left.append(value * scale[s])
                target = jnp.where(inside, 0.0, target)
                for s in range(8):
                    target = target - left[s] * solved[s]
                groups[other] = target
        if quarter < 3:
            at = 32 * quarter
            inside = (lane >= at) & (lane < at + 32)
            rows = jnp.concatenate(
                [
                    jnp.where(inside & (lane > 8 * g + row), 0.0, groups[g])
                    for g in range(first, first + 4)
                ],
                axis=0,
            )
            turned = rows.T[at + 32:, :]
            high, low = split(rows)
            turned_high, turned_low = split(turned)
            change = dot(turned_high, high) + dot(turned_low, high) + dot(turned_high, low)
            for other in range(first + 4, 16):
                begin = (other - first - 4) * 8
                groups[other] = jnp.where(inside, 0.0, groups[other]) - change[begin:begin + 8, :]
    return [jnp.where(lane > 8 * g + row, 0.0, groups[g]) for g in range(16)]


class Leave:
    def __init__(self, ready, beside, landed, sems, spot):
        self.ready, self.beside, self.landed = ready, beside, landed
        self.p_send, self.p_recv, self.z_send, self.z_recv, self.local = sems
        self.x, self.y, self.z, self.core = spot

    def pair(self, k):
        return remote(
            self.ready.at[k, 1 - self.core], self.beside.at[k], self.p_send.at[k], self.p_recv.at[k],
            device(self.x, self.y, self.z, 1 - self.core),
        )

    def source(self, path, k, part):
        return self.ready.at[k, self.core, part] if path == 0 else self.beside.at[k, part]

    def origin(self, path):
        return self.core if path == 0 else 1 - self.core

    def along(self, path, k, part):
        return remote(
            self.source(path, k, part), self.landed.at[self.z, self.origin(path)],
            self.z_send.at[path, 2 * k + part], self.z_recv.at[path, self.z],
            device(self.x, self.y, 2 * k + part, self.core),
        )

    def keep(self, path, k, part):
        return pltpu.make_async_copy(
            self.source(path, k, part), self.landed.at[self.z, self.origin(path)], self.local.at[path]
        )

    def start(self, path, k):
        if path == 1:
            self.pair(k).wait_recv()
        for part in range(2):

            @pl.when(self.z != 2 * k + part)
            def _():
                self.along(path, k, part).start()

            @pl.when(self.z == 2 * k + part)
            def _():
                self.keep(path, k, part).start()

    def finish(self):
        for path in range(2):
            for step in range(1, Z):
                source = lax.rem(self.z + step, Z)
                spot = self.landed.at[source, self.origin(path)]
                remote(
                    spot, spot, self.z_send.at[path, source], self.z_recv.at[path, source],
                    device(self.x, self.y, source, self.core),
                ).wait_recv()
            for k in range(BLOCKS):
                for part in range(2):

                    @pl.when(self.z != 2 * k + part)
                    def _():
                        self.along(path, k, part).wait_send()

                    @pl.when(self.z == 2 * k + part)
                    def _():
                        self.keep(path, k, part).wait()
        for k in range(BLOCKS):
            self.pair(k).wait_send()


def solve(gram, products, landed, mat, ready, beside, sems, spot):
    leave = Leave(ready, beside, landed, sems, spot)
    lane = lax.broadcasted_iota(jnp.int32, (8, 128), 1)
    row = lax.broadcasted_iota(jnp.int32, (8, 128), 0)
    count = 0
    for rows in ROWS_OF_CORE:
        for i in rows:
            for j in range(i, BLOCKS):
                mat[i * BLOCK:(i + 1) * BLOCK, j * BLOCK:(j + 1) * BLOCK] = (
                    gram[count * 16:(count + 1) * 16].reshape(BLOCK, BLOCK) * (1.0 / 131072.0)
                )
                count += 1
            if i:
                mat[i * BLOCK:(i + 1) * BLOCK, :i * BLOCK] = jnp.zeros((BLOCK, i * BLOCK), jnp.float32)

    def step(k, carry):
        begin = pl.multiple_of(k * BLOCK, BLOCK)
        own = pl.ds(begin, BLOCK)

        def load(g):
            return mat[pl.ds(pl.multiple_of(begin + 8 * g, 8), 8), own]

        for g, value in enumerate(factor_block(load, lane, row)):
            mat[pl.ds(pl.multiple_of(begin + 8 * g, 8), 8), own] = value
        for kk in range(BLOCKS):

            @pl.when(k == kk)
            def _():
                at = kk * BLOCK
                high, low = split(mat[at:at + BLOCK, at:at + BLOCK])
                left = jnp.concatenate([high, low], axis=1)
                spans = [(0, at), (at + BLOCK, NB)]
                for start, stop in spans:
                    if start < stop:
                        up, down = split(mat[at:at + BLOCK, start:stop])
                        mat[at:at + BLOCK, start:stop] = dot(left, jnp.concatenate([up, up], axis=0)) + dot(high, down)
                inverse = jnp.concatenate(
                    [
                        mat[at + 64 * to_z + 16 * to_y + 8 * to_core:at + 64 * to_z + 16 * to_y + 8 * to_core + 8, :at + BLOCK]
                        for to_core in range(CORES)
                        for to_z in range(2)
                        for to_y in range(Y)
                    ],
                    axis=0,
                ).astype(jnp.bfloat16)
                local = dot(inverse, products[:at + BLOCK, :]).astype(jnp.bfloat16)
                for to_core in range(CORES):
                    for to_z in range(2):
                        first = 64 * to_core + 32 * to_z
                        ready[kk, to_core, to_z] = local[first:first + 32, :]
                leave.pair(kk).start()
                leave.start(0, kk)
                if kk + 1 < BLOCKS:
                    after = at + BLOCK
                    turned_high, turned_low = split(mat[at:at + BLOCK, after:].T)
                    turned = jnp.concatenate([turned_high, turned_low], axis=1)
                    for start in range(0, NB, 256):
                        up, down = split(mat[at:at + BLOCK, start:start + 256])
                        change = dot(turned, jnp.concatenate([up, up], axis=0)) + dot(turned_high, down)
                        if start <= at < start + 256:
                            for part in (start, start + BLOCK):
                                piece = change[:, part - start:part - start + BLOCK]
                                if part == at:
                                    mat[after:, part:part + BLOCK] = -piece
                                else:
                                    mat[after:, part:part + BLOCK] = mat[after:, part:part + BLOCK] - piece
                        else:
                            mat[after:, start:start + 256] = mat[after:, start:start + 256] - change
                leave.start(1, kk)

        return carry

    lax.fori_loop(0, BLOCKS, step, 0)
    leave.finish()


def pick(orbitals, pivots):
    folded = orbitals.reshape(2, 1024, 128)
    outer = (pivots[:, None] // 128 == jnp.arange(1024, dtype=jnp.int32)[None, :]).astype(jnp.bfloat16)
    inner = pivots[:, None] % 128 == jnp.arange(128, dtype=jnp.int32)[None, :]
    rows = jnp.einsum("jh,rhl->rjl", outer, folded, preferred_element_type=jnp.float32)
    return jnp.sum(jnp.where(inner[None], rows, 0.0), axis=2).astype(jnp.bfloat16)


def body(orbitals, pivots):
    points = orbitals.shape[1] // 512
    entries = (Z, Y, CORES, X, 2, points)
    piece = pick(orbitals, pivots).reshape(16, 128)
    outgoing = orbitals.reshape(2, 512, points).transpose(1, 0, 2).reshape(entries)
    slab, rows = gather(outgoing, piece)
    products = (
        lax.dot_general(
            rows.reshape(NB, NB), slab.reshape(NB, points), (((0,), (0,)), ((), ())),
            preferred_element_type=jnp.float32,
        )
        * (1.0 / math.sqrt(NB))
    ).astype(jnp.bfloat16)
    landed = localize(products)
    returned = give_back(landed.reshape(Z, CORES, Y, X, 2, points))
    return returned.reshape(512, 2, points).transpose(1, 0, 2).reshape(orbitals.shape)


def solution(mesh):
    placed = (P(("grid", "band"), None), P())
    return jax.shard_map(
        body, mesh=mesh, in_specs=placed, out_specs=P(("grid", "band"), None), check_vma=False
    )
```

```python
import functools
import math

import jax
import jax.numpy as jnp
from jax import lax
from jax.experimental import pallas as pl
from jax.experimental.pallas import tpu as pltpu
from jax.sharding import PartitionSpec as P

MESH = pl.DeviceIdType.MESH
X, Y, Z, CORES = 4, 4, 16, 2
NB = 1024
BLOCK = 128
BLOCKS = NB // BLOCK
TILES = 576
OWNERS = 9
ROWS_OF_CORE = ((0, 3, 4, 7), (1, 2, 5, 6))
VMEM = 48 * 1024 * 1024


def place():
    grid = lax.axis_index("grid")
    return lax.axis_index("band"), lax.rem(grid // CORES, Y), grid // (CORES * Y), lax.rem(grid, CORES)


def device(x, y, z, core):
    return ((z * Y + y) * CORES + core, x)


def greet(x, y, z, core, plane):
    barrier = pltpu.get_barrier_semaphore()
    partners = [device(x, y, z, 1 - core)]
    for along_y in range(Y):
        for along_x in range(X):
            if (along_x or along_y) and (plane or not (along_x and along_y)):
                partners.append(device(lax.rem(x + along_x, X), lax.rem(y + along_y, Y), z, core))
    for step in range(1, Z):
        partners.append(device(x, y, lax.rem(z + step, Z), core))
    for partner in partners:
        pl.semaphore_signal(barrier, inc=1, device_id=partner, device_id_type=MESH)
    pl.semaphore_wait(barrier, len(partners))


def remote(src, dst, send, recv, target):
    return pltpu.make_async_remote_copy(
        src_ref=src, dst_ref=dst, send_sem=send, recv_sem=recv, device_id=target, device_id_type=MESH
    )


def spread(out, unit, x, y, z, core, send, recv):
    half = 16 * unit
    base = core * 2 * half
    firsts = (x, y)
    seconds = (y, x)

    def mate(axis_is_x, step):
        if axis_is_x:
            return device(lax.rem(x + step, X), y, z, core)
        return device(x, lax.rem(y + step, Y), z, core)

    started = []
    inner = []
    for h in range(2):
        mine = out.at[pl.ds(base + h * half + (firsts[h] * 4 + seconds[h]) * unit, unit)]
        for step in range(1, 4):
            copy = remote(mine, mine, send.at[0, h, step], recv.at[0, h, step], mate(h == 1, step))
            copy.start()
            inner.append(copy)
    for copy in inner:
        copy.wait_recv()
    started += inner
    sibling = device(x, y, z, 1 - core)
    across = []
    near = []
    block = 4 * unit

    def part(h, where, begin=0, size=block):
        return out.at[pl.ds(base + h * half + lax.rem(firsts[h] + where, 4) * block + begin, size)]

    def forward(h, index, ref):
        copy = remote(ref, ref, send.at[2, h, index], recv.at[2, h, index], sibling)
        copy.start()
        across.append(copy)

    for h in range(2):
        for index, step in ((0, 1), (1, 3)):
            copy = remote(part(h, 0), part(h, 0), send.at[1, h, index], recv.at[1, h, index], mate(h == 0, step))
            copy.start()
            near.append((h, index, step, copy))
    for h in range(2):
        forward(h, 0, part(h, 0))
    far = []
    for h, index, step, copy in near:
        copy.wait_recv()
        ref = part(h, 4 - step, index * (block // 2), block // 2)
        onward = remote(ref, ref, send.at[1, h, 2 + index], recv.at[1, h, 2 + index], mate(h == 0, step))
        onward.start()
        far.append(onward)
        forward(h, 1 + index, part(h, 4 - step))
        started.append(copy)
    for copy in far:
        copy.wait_recv()
    for h in range(2):
        forward(h, 3, part(h, 2))
    for copy in across:
        copy.wait_recv()
    for copy in started + far + across:
        copy.wait_send()


def order_of_z():
    steps = []
    for step in range(1, Z // 2 + 1):
        steps.append(step)
        if step != Z - step:
            steps.append(Z - step)
    return steps


class Regroup:
    def __init__(self, source, out, beside, landed, sems, spot):
        self.source, self.out, self.beside, self.landed = source, out, beside, landed
        self.p_send, self.p_recv, self.z_send, self.z_recv, self.y_send, self.y_recv, self.local = sems
        self.x, self.y, self.z, self.core = spot
        self.origin = (self.core, 1 - self.core)
        self.pair = remote(
            source.at[:, :, 1 - self.core], beside, self.p_send, self.p_recv,
            device(self.x, self.y, self.z, 1 - self.core),
        )
        self.done = []
        self.paths = []
        self.plane = []

    def leaving(self, path, z):
        return self.source.at[z, :, self.core] if path == 0 else self.beside.at[z]

    def start_z(self, path):
        x, y, z, core = self.x, self.y, self.z, self.core
        if path == 1:
            self.pair.wait_recv()
        landing = self.landed.at[self.origin[path], z]
        copies = []
        for step in order_of_z():
            target = lax.rem(z + step, Z)
            copy = remote(
                self.leaving(path, target), landing, self.z_send.at[path, step], self.z_recv.at[path, step],
                device(x, y, target, core),
            )
            copy.start()
            copies.append(copy)
        own = pltpu.make_async_copy(self.leaving(path, z), landing, self.local.at[path])
        own.start()
        self.paths.append((own, copies))

    def start_plane(self, path):
        x, y, z, core = self.x, self.y, self.z, self.core
        own, copies = self.paths[path]
        own.wait()
        for copy in copies:
            copy.wait_recv()
        self.done += copies
        origin = self.origin[path]
        landing = self.out.at[:, y, origin, x]
        for along_y in range(Y):
            for along_x in range(X):
                if along_x or along_y:
                    to_x, to_y = lax.rem(x + along_x, X), lax.rem(y + along_y, Y)
                    index = along_y * X + along_x
                    copy = remote(
                        self.landed.at[origin, :, to_y, to_x], landing,
                        self.y_send.at[path, index], self.y_recv.at[path, index],
                        device(to_x, to_y, z, core),
                    )
                    copy.start()
                    self.plane.append(copy)
        keep = pltpu.make_async_copy(self.landed.at[origin, :, y, x], landing, self.local.at[2 + path])
        keep.start()
        self.done_keep = getattr(self, "done_keep", []) + [keep]

    def finish(self):
        for copy in self.plane:
            copy.wait_recv()
        for keep in self.done_keep:
            keep.wait()
        for copy in self.plane + self.done + [self.pair]:
            copy.wait_send()


def gather_part(orbitals, piece, slab, rows, across, beside, landed, moving, sems, spot):
    q_send, q_recv, send, recv = sems
    x, y, z, core = spot
    regroup = Regroup(orbitals, slab, beside, landed, moving, (x, y, z, core))
    regroup.pair.start()
    first = []
    for step in order_of_z():
        copy = remote(
            piece, rows.at[z, y, core, x], q_send.at[step], q_recv.at[step], device(x, y, lax.rem(z + step, Z), core)
        )
        copy.start()
        first.append(copy)
    regroup.start_z(0)
    regroup.start_z(1)
    rows[z, y, core, x] = piece[...]
    for copy in first:
        copy.wait_recv()
    second = []
    mine = rows.at[:, y, core, x]
    for step in range(1, Y):
        copy = remote(
            mine, mine, send.at[0, step], recv.at[0, step], device(x, lax.rem(y + step, Y), z, core)
        )
        copy.start()
        second.append(copy)
    for copy in second:
        copy.wait_recv()
    sibling = device(x, y, z, 1 - core)
    near, far, last = [], [], []

    def along_x(step):
        return device(lax.rem(x + step, X), y, z, core)

    def forward(index, ref):
        copy = remote(ref, ref, send.at[2, index], recv.at[2, index], sibling)
        copy.start()
        last.append(copy)

    mine = rows.at[:, :, core, x]
    for index, step in ((0, 1), (1, 3)):
        copy = remote(mine, mine, send.at[1, index], recv.at[1, index], along_x(step))
        copy.start()
        near.append(copy)
    forward(0, mine)
    for index, step in ((0, 1), (1, 3)):
        near[index].wait_recv()
        source = lax.rem(x + 4 - step, X)
        ref = rows.at[pl.ds(index * (Z // 2), Z // 2), :, core, source]
        copy = remote(ref, ref, send.at[1, 2 + index], recv.at[1, 2 + index], along_x(step))
        copy.start()
        far.append(copy)
        forward(1 + index, rows.at[:, :, core, source])
    regroup.start_plane(0)
    for copy in far:
        copy.wait_recv()
    forward(3, rows.at[:, :, core, lax.rem(x + 2, X)])
    for copy in last:
        copy.wait_recv()
    for part in range(BLOCKS):
        block = rows[2 * part:2 * part + 2].reshape(64, 16, 128).reshape(128, 8, 128).reshape(128, NB)
        across[:, part * BLOCK:(part + 1) * BLOCK] = block.T
    regroup.start_plane(1)
    regroup.finish()
    for copy in first + second + near + far + last:
        copy.wait_send()


def plane_part(landed, ordered, out, arrive, sems, spot):
    send, recv, kept = sems
    x, y, z, core = spot
    copies = []
    keeps = []
    for turn, offset in enumerate((0, 1, 3, 2)):
        first = lax.rem(z // 4 + offset, 4) * 4
        for step in range(4):
            arrive(first + step)
        group = pl.ds(first, 4)
        ordered[group] = landed[group].reshape(4, CORES, Y, X, 2, landed.shape[-1])
        landing = out.at[group, y, :, x]
        for along_y in range(Y):
            for along_x in range(X):
                if along_x or along_y:
                    to_x, to_y = lax.rem(x + along_x, X), lax.rem(y + along_y, Y)
                    index = along_y * X + along_x
                    copy = remote(
                        ordered.at[group, :, to_y, to_x], landing, send.at[turn, index], recv.at[turn, index],
                        device(to_x, to_y, z, core),
                    )
                    copy.start()
                    copies.append(copy)
        keep = pltpu.make_async_copy(ordered.at[group, :, y, x], landing, kept.at[turn])
        keep.start()
        keeps.append(keep)
    for copy in copies:
        copy.wait_recv()
    for copy in copies:
        copy.wait_send()
    for keep in keeps:
        keep.wait()


def gram_part(across, slab, products, out, theirs, terms, got0, got1, got2, got3, sems, spot):
    send, recv, r_send, r_recv, z_send, z_recv, g_send, g_recv, p_send, p_recv = sems
    x, y, z, core = spot
    pairs = []
    columns = slab[...].reshape(NB, slab.shape[-1])
    for part in range(4):
        rows = slice(part * 256, (part + 1) * 256)
        products[rows, :] = (dot(across[rows, :], columns) * (1.0 / math.sqrt(NB))).astype(jnp.bfloat16)
        pair = remote(
            products.at[rows, :], theirs.at[rows, :], p_send.at[part], p_recv.at[part], device(x, y, z, 1 - core)
        )
        pair.start()
        pairs.append(pair)
    contract = (((1,), (1,)), ((), ()))

    def add(source, again):
        for which in range(CORES):

            @pl.when(core == which)
            def _():
                count = 0
                for i in ROWS_OF_CORE[which]:
                    row = lax.dot_general(
                        source[i * BLOCK:(i + 1) * BLOCK, :], source[i * BLOCK:, :], contract,
                        preferred_element_type=jnp.float32,
                    )
                    for j in range(BLOCKS - i):
                        tiles = slice(count * 16, (count + 1) * 16)
                        term = row[:, j * BLOCK:(j + 1) * BLOCK].reshape(16, 8, 128)
                        terms[tiles] = terms[tiles] + term if again else term
                        count += 1

    add(products, False)
    for pair in pairs:
        pair.wait_recv()
    add(theirs, True)

    unit = OWNERS
    half = 16 * unit
    firsts = (x, y)
    seconds = (y, x)

    def mate(axis_is_x, step):
        if axis_is_x:
            return device(lax.rem(x + step, X), y, z, core)
        return device(x, lax.rem(y + step, Y), z, core)

    block = 4 * unit
    middle = block // 2

    def span(h, where, begin=0, size=block):
        return pl.ds(h * half + lax.rem(firsts[h] + where, 4) * block + begin, size)

    copies = []
    for h in range(2):
        for index, step in ((0, 1), (1, 3)):
            copy = remote(
                terms.at[span(h, 2, index * middle, middle)], got0.at[h, index],
                r_send.at[0, h, index], r_recv.at[0, h, index], mate(h == 0, step),
            )
            copy.start()
            copies.append((h, index, step, copy))
    near = []
    for h, index, step, copy in copies:
        copy.wait_recv()
        part = span(h, step, index * middle, middle)
        terms[part] = terms[part] + got0[h, index]
        onward = remote(
            terms.at[span(h, step)], got1.at[h, index], r_send.at[2, h, index], r_recv.at[2, h, index],
            mate(h == 0, step),
        )
        onward.start()
        near.append(onward)
    copies = [copy for _, _, _, copy in copies] + near
    for copy in near:
        copy.wait_recv()
    for h in range(2):
        mine = span(h, 0)
        terms[mine] = terms[mine] + (got1[h, 0] + got1[h, 1])
    later = []
    for step in range(1, 4):
        for h in range(2):
            target = lax.rem(seconds[h] + step, 4)
            copy = remote(
                terms.at[pl.ds(h * half + (firsts[h] * 4 + target) * unit, unit)],
                got2.at[h, step - 1],
                r_send.at[1, h, step],
                r_recv.at[1, h, step],
                mate(h == 1, step),
            )
            copy.start()
            later.append(copy)
    for copy in later:
        copy.wait_recv()
    starts = [h * half + (firsts[h] * 4 + seconds[h]) * unit for h in range(2)]
    for h in range(2):
        mine = pl.ds(starts[h], unit)
        terms[mine] = terms[mine] + (got2[h, 0] + got2[h, 1]) + got2[h, 2]

    def to_owner(step, h):
        target = lax.rem(z + step, Z)
        tile = jnp.minimum(target, OWNERS - 1)
        return target, remote(
            terms.at[starts[h] + tile],
            got3.at[step - 1, h],
            z_send.at[step, h],
            z_recv.at[step, h],
            device(x, y, target, core),
        )

    for step in range(1, Z):
        for h in range(2):
            target, copy = to_owner(step, h)

            @pl.when(target < OWNERS)
            def _():
                copy.start()

    goals = [core * 2 * half + starts[h] for h in range(2)]
    tile = jnp.minimum(z, OWNERS - 1)

    def to_all(step, h):
        return remote(
            out.at[goals[h] + tile],
            out.at[goals[h] + tile],
            g_send.at[step, h],
            g_recv.at[step, h],
            device(x, y, lax.rem(z + step, Z), core),
        )

    @pl.when(z < OWNERS)
    def _():
        for step in range(1, Z):
            for h in range(2):
                to_owner(step, h)[1].wait_recv()
        for h in range(2):
            total = terms[starts[h] + tile]
            for step in range(1, Z):
                total = total + got3[step - 1, h]
            out[goals[h] + tile] = total
        for step in range(1, Z):
            for h in range(2):
                to_all(step, h).start()

    for step in range(1, Z):
        source = lax.rem(z + Z - step, Z)

        @pl.when(source < OWNERS)
        def _():
            for h in range(2):
                to_all(step, h).wait_recv()

    spread(out, unit, x, y, z, core, send, recv)

    for step in range(1, Z):
        for h in range(2):
            target, copy = to_owner(step, h)

            @pl.when(target < OWNERS)
            def _():
                copy.wait_send()

    @pl.when(z < OWNERS)
    def _():
        for step in range(1, Z):
            for h in range(2):
                to_all(step, h).wait_send()

    for copy in copies + later + pairs:
        copy.wait_send()


def split(value):
    high = value.astype(jnp.bfloat16)
    return high, (value - high.astype(jnp.float32)).astype(jnp.bfloat16)


def dot(a, b):
    return jnp.dot(a, b, preferred_element_type=jnp.float32)


def factor_block(load, lane, row):
    full = (8, 128)
    groups = [load(g) for g in range(16)]
    for quarter in range(4):
        first = 4 * quarter
        for g in range(first, first + 4):
            at = 8 * g
            panel = groups[g]
            columns = [jnp.broadcast_to(panel[:, at + t:at + t + 1], full) for t in range(8)]
            a = [[jnp.broadcast_to(columns[t][i:i + 1, :], full) for t in range(i + 1)] for i in range(8)]
            below = [[None] * 8 for _ in range(8)]
            scale = []
            for s in range(8):
                r = lax.rsqrt(a[s][s])
                scale.append(r)
                for i in range(s + 1, 8):
                    below[i][s] = a[i][s] * r
                for i in range(s + 1, 8):
                    for t in range(s + 1, i + 1):
                        a[i][t] = a[i][t] - below[i][s] * below[t][s]
            inside = (lane >= at) & (lane < at + 8)
            panel = jnp.where(inside, (lane == row + at).astype(jnp.float32), panel)
            solved = []
            for s in range(8):
                value = jnp.broadcast_to(panel[s:s + 1, :], full)
                for t in range(s):
                    value = value - below[s][t] * solved[t]
                solved.append(value * scale[s])
            result = solved[0]
            for s in range(1, 8):
                result = jnp.where(row == s, solved[s], result)
            groups[g] = result
            for other in range(g + 1, first + 4):
                target = groups[other]
                left = []
                for s in range(8):
                    value = jnp.broadcast_to(target[:, at + s:at + s + 1], full)
                    for t in range(s):
                        value = value - below[s][t] * left[t]
                    left.append(value * scale[s])
                target = jnp.where(inside, 0.0, target)
                for s in range(8):
                    target = target - left[s] * solved[s]
                groups[other] = target
        if quarter < 3:
            at = 32 * quarter
            inside = (lane >= at) & (lane < at + 32)
            rows = jnp.concatenate(
                [
                    jnp.where(inside & (lane > 8 * g + row), 0.0, groups[g])
                    for g in range(first, first + 4)
                ],
                axis=0,
            )
            turned = rows.T[at + 32:, :]
            high, low = split(rows)
            turned_high, turned_low = split(turned)
            change = dot(turned_high, high) + dot(turned_low, high) + dot(turned_high, low)
            for other in range(first + 4, 16):
                begin = (other - first - 4) * 8
                groups[other] = jnp.where(inside, 0.0, groups[other]) - change[begin:begin + 8, :]
    return [jnp.where(lane > 8 * g + row, 0.0, groups[g]) for g in range(16)]


class Leave:
    def __init__(self, ready, beside, landed, sems, spot):
        self.ready, self.beside, self.landed = ready, beside, landed
        self.p_send, self.p_recv, self.z_send, self.z_recv, self.local = sems
        self.x, self.y, self.z, self.core = spot

    def pair(self, k):
        return remote(
            self.ready.at[k, 1 - self.core], self.beside.at[k], self.p_send.at[k], self.p_recv.at[k],
            device(self.x, self.y, self.z, 1 - self.core),
        )

    def source(self, path, k, part):
        return self.ready.at[k, self.core, part] if path == 0 else self.beside.at[k, part]

    def origin(self, path):
        return self.core if path == 0 else 1 - self.core

    def along(self, path, k, part):
        return remote(
            self.source(path, k, part), self.landed.at[self.z, self.origin(path)],
            self.z_send.at[path, 2 * k + part], self.z_recv.at[path, self.z],
            device(self.x, self.y, 2 * k + part, self.core),
        )

    def keep(self, path, k, part):
        return pltpu.make_async_copy(
            self.source(path, k, part), self.landed.at[self.z, self.origin(path)], self.local.at[path]
        )

    def start(self, path, k):
        if path == 1:
            self.pair(k).wait_recv()
        for part in range(2):

            @pl.when(self.z != 2 * k + part)
            def _():
                self.along(path, k, part).start()

            @pl.when(self.z == 2 * k + part)
            def _():
                self.keep(path, k, part).start()

    def arrive(self, source):
        @pl.when(self.z != source)
        def _():
            for path in range(2):
                spot = self.landed.at[source, self.origin(path)]
                remote(
                    spot, spot, self.z_send.at[path, source], self.z_recv.at[path, source],
                    device(self.x, self.y, source, self.core),
                ).wait_recv()

        @pl.when(self.z == source)
        def _():
            for path in range(2):
                spot = self.landed.at[source, self.origin(path)]
                pltpu.make_async_copy(spot, spot, self.local.at[path]).wait()

    def finish(self):
        for path in range(2):
            for k in range(BLOCKS):
                for part in range(2):

                    @pl.when(self.z != 2 * k + part)
                    def _():
                        self.along(path, k, part).wait_send()

        for k in range(BLOCKS):
            self.pair(k).wait_send()


def solve(gram, products, mat, leave):
    ready = leave.ready
    lane = lax.broadcasted_iota(jnp.int32, (8, 128), 1)
    row = lax.broadcasted_iota(jnp.int32, (8, 128), 0)
    count = 0
    for rows in ROWS_OF_CORE:
        for i in rows:
            for j in range(i, BLOCKS):
                mat[i * BLOCK:(i + 1) * BLOCK, j * BLOCK:(j + 1) * BLOCK] = (
                    gram[count * 16:(count + 1) * 16].reshape(BLOCK, BLOCK) * (1.0 / 131072.0)
                )
                count += 1
            if i:
                mat[i * BLOCK:(i + 1) * BLOCK, :i * BLOCK] = jnp.zeros((BLOCK, i * BLOCK), jnp.float32)

    def step(k, carry):
        begin = pl.multiple_of(k * BLOCK, BLOCK)
        own = pl.ds(begin, BLOCK)

        def load(g):
            return mat[pl.ds(pl.multiple_of(begin + 8 * g, 8), 8), own]

        for g, value in enumerate(factor_block(load, lane, row)):
            mat[pl.ds(pl.multiple_of(begin + 8 * g, 8), 8), own] = value
        for kk in range(BLOCKS):

            @pl.when(k == kk)
            def _():
                at = kk * BLOCK
                high, low = split(mat[at:at + BLOCK, at:at + BLOCK])
                left = jnp.concatenate([high, low], axis=1)
                spans = [(0, at), (at + BLOCK, NB)]
                for start, stop in spans:
                    if start < stop:
                        up, down = split(mat[at:at + BLOCK, start:stop])
                        mat[at:at + BLOCK, start:stop] = dot(left, jnp.concatenate([up, up], axis=0)) + dot(high, down)
                inverse = jnp.concatenate(
                    [
                        mat[at + 64 * to_z + 16 * to_y + 8 * to_core:at + 64 * to_z + 16 * to_y + 8 * to_core + 8, :at + BLOCK]
                        for to_core in range(CORES)
                        for to_z in range(2)
                        for to_y in range(Y)
                    ],
                    axis=0,
                ).astype(jnp.bfloat16)
                local = dot(inverse, products[:at + BLOCK, :]).astype(jnp.bfloat16)
                for to_core in range(CORES):
                    for to_z in range(2):
                        first = 64 * to_core + 32 * to_z
                        ready[kk, to_core, to_z] = local[first:first + 32, :]
                leave.pair(kk).start()
                leave.start(0, kk)
                if kk + 1 < BLOCKS:
                    after = at + BLOCK
                    turned_high, turned_low = split(mat[at:at + BLOCK, after:].T)
                    turned = jnp.concatenate([turned_high, turned_low], axis=1)
                    for start in range(0, NB, 256):
                        up, down = split(mat[at:at + BLOCK, start:start + 256])
                        change = dot(turned, jnp.concatenate([up, up], axis=0)) + dot(turned_high, down)
                        if start <= at < start + 256:
                            for part in (start, start + BLOCK):
                                piece = change[:, part - start:part - start + BLOCK]
                                if part == at:
                                    mat[after:, part:part + BLOCK] = -piece
                                else:
                                    mat[after:, part:part + BLOCK] = mat[after:, part:part + BLOCK] - piece
                        else:
                            mat[after:, start:start + 256] = mat[after:, start:start + 256] - change
                leave.start(1, kk)

        return carry

    lax.fori_loop(0, BLOCKS, step, 0)


def whole_kernel(orbitals, piece, out, *scratch):
    buffers, sems = scratch[:BUFFERS], scratch[BUFFERS:]
    (
        beside, landed, slab, rows, across, products, gram, theirs, terms, got0, got1, got2, got3,
        mat, ready, beside2, landed2, ordered,
    ) = buffers
    spot = place()
    greet(*spot, True)
    gather_part(orbitals, piece, slab, rows, across, beside, landed, sems[:7], sems[7:11], spot)
    gram_part(across, slab, products, gram, theirs, terms, got0, got1, got2, got3, sems[11:21], spot)
    leave = Leave(ready, beside2, landed2, sems[21:26], spot)
    solve(gram, products, mat, leave)
    plane_part(landed2, ordered, out, leave.arrive, sems[26:29], spot)
    leave.finish()


BUFFERS = 18


def whole(orbitals, piece):
    points = orbitals.shape[-1]
    unit = OWNERS
    dma = pltpu.SemaphoreType.DMA
    narrow, wide = jnp.bfloat16, jnp.float32
    entries = (Z, Y, CORES, X, 2, points)
    held = Y * X * 2
    buffers = [
        pltpu.VMEM((Z, Y, X, 2, points), narrow),
        pltpu.VMEM((CORES, Z, Y, X, 2, points), narrow),
        pltpu.VMEM(entries, narrow),
        pltpu.VMEM((Z, Y, CORES, X, 16, 128), narrow),
        pltpu.VMEM((NB, NB), narrow),
        pltpu.VMEM((NB, points), narrow),
        pltpu.VMEM((TILES, 8, 128), wide),
        pltpu.VMEM((NB, points), narrow),
        pltpu.VMEM((TILES // 2, 8, 128), wide),
        pltpu.VMEM((2, 2, 2 * unit, 8, 128), wide),
        pltpu.VMEM((2, 2, 4 * unit, 8, 128), wide),
        pltpu.VMEM((2, 3, unit, 8, 128), wide),
        pltpu.VMEM((Z - 1, 2, 8, 128), wide),
        pltpu.VMEM((NB, NB), wide),
        pltpu.VMEM((BLOCKS, CORES, 2, held, points), narrow),
        pltpu.VMEM((BLOCKS, 2, held, points), narrow),
        pltpu.VMEM((Z, CORES, held, points), narrow),
        pltpu.VMEM((Z, CORES, Y, X, 2, points), narrow),
    ]
    sems = [
        dma, dma, dma((2, Z)), dma((2, Z)), dma((2, X * Y)), dma((2, X * Y)), dma((4,)),
        dma((Z,)), dma((Z,)), dma((3, 4)), dma((3, 4)),
        dma((3, 2, 4)), dma((3, 2, 4)), dma((3, 2, 4)), dma((3, 2, 4)),
        dma((Z, 2)), dma((Z, 2)), dma((Z, 2)), dma((Z, 2)), dma((4,)), dma((4,)),
        dma((BLOCKS,)), dma((BLOCKS,)), dma((2, Z)), dma((2, Z)), dma((2,)),
        dma((4, X * Y)), dma((4, X * Y)), dma((4,)),
    ]
    return pl.pallas_call(
        whole_kernel,
        out_shape=jax.ShapeDtypeStruct(entries, narrow),
        in_specs=[pl.BlockSpec(memory_space=pltpu.VMEM)] * 2,
        out_specs=pl.BlockSpec(memory_space=pltpu.VMEM),
        scratch_shapes=buffers + sems,
        compiler_params=pltpu.CompilerParams(collective_id=0, has_side_effects=True, vmem_limit_bytes=VMEM),
        name="localize",
    )(orbitals, piece)


def pick(orbitals, pivots):
    folded = orbitals.reshape(2, 1024, 128)
    outer = (pivots[:, None] // 128 == jnp.arange(1024, dtype=jnp.int32)[None, :]).astype(jnp.bfloat16)
    inner = pivots[:, None] % 128 == jnp.arange(128, dtype=jnp.int32)[None, :]
    rows = jnp.einsum("jh,rhl->rjl", outer, folded, preferred_element_type=jnp.float32)
    return jnp.sum(jnp.where(inner[None], rows, 0.0), axis=2).astype(jnp.bfloat16)


def body(orbitals, pivots):
    points = orbitals.shape[1] // 512
    entries = (Z, Y, CORES, X, 2, points)
    piece = pick(orbitals, pivots).reshape(16, 128)
    outgoing = orbitals.reshape(2, 512, points).transpose(1, 0, 2).reshape(entries)
    returned = whole(outgoing, piece)
    return returned.reshape(512, 2, points).transpose(1, 0, 2).reshape(orbitals.shape)


def solution(mesh):
    placed = (P(("grid", "band"), None), P())
    return jax.shard_map(
        body, mesh=mesh, in_specs=placed, out_specs=P(("grid", "band"), None), check_vma=False
    )
```

```python
import functools
import math

import jax
import jax.numpy as jnp
from jax import lax
from jax.experimental import pallas as pl
from jax.experimental.pallas import tpu as pltpu
from jax.sharding import PartitionSpec as P

MESH = pl.DeviceIdType.MESH
X, Y, Z, CORES = 4, 4, 16, 2
NB = 1024
BLOCK = 128
BLOCKS = NB // BLOCK
TILES = 576
OWNERS = 9
ROWS_OF_CORE = ((0, 3, 4, 7), (1, 2, 5, 6))
VMEM = 48 * 1024 * 1024


def place():
    grid = lax.axis_index("grid")
    return lax.axis_index("band"), lax.rem(grid // CORES, Y), grid // (CORES * Y), lax.rem(grid, CORES)


def device(x, y, z, core):
    return ((z * Y + y) * CORES + core, x)


def greet(x, y, z, core, plane):
    barrier = pltpu.get_barrier_semaphore()
    partners = [device(x, y, z, 1 - core)]
    for along_y in range(Y):
        for along_x in range(X):
            if (along_x or along_y) and (plane or not (along_x and along_y)):
                partners.append(device(lax.rem(x + along_x, X), lax.rem(y + along_y, Y), z, core))
    for step in range(1, Z):
        partners.append(device(x, y, lax.rem(z + step, Z), core))
    for partner in partners:
        pl.semaphore_signal(barrier, inc=1, device_id=partner, device_id_type=MESH)
    pl.semaphore_wait(barrier, len(partners))


def remote(src, dst, send, recv, target):
    return pltpu.make_async_remote_copy(
        src_ref=src, dst_ref=dst, send_sem=send, recv_sem=recv, device_id=target, device_id_type=MESH
    )


def spread(out, unit, x, y, z, core, send, recv):
    half = 16 * unit
    base = core * 2 * half
    firsts = (x, y)
    seconds = (y, x)

    def mate(axis_is_x, step):
        if axis_is_x:
            return device(lax.rem(x + step, X), y, z, core)
        return device(x, lax.rem(y + step, Y), z, core)

    started = []
    inner = []
    for h in range(2):
        mine = out.at[pl.ds(base + h * half + (firsts[h] * 4 + seconds[h]) * unit, unit)]
        for step in range(1, 4):
            copy = remote(mine, mine, send.at[0, h, step], recv.at[0, h, step], mate(h == 1, step))
            copy.start()
            inner.append(copy)
    for copy in inner:
        copy.wait_recv()
    started += inner
    sibling = device(x, y, z, 1 - core)
    across = []
    near = []
    block = 4 * unit

    def part(h, where, begin=0, size=block):
        return out.at[pl.ds(base + h * half + lax.rem(firsts[h] + where, 4) * block + begin, size)]

    def forward(h, index, ref):
        copy = remote(ref, ref, send.at[2, h, index], recv.at[2, h, index], sibling)
        copy.start()
        across.append(copy)

    for h in range(2):
        for index, step in ((0, 1), (1, 3)):
            copy = remote(part(h, 0), part(h, 0), send.at[1, h, index], recv.at[1, h, index], mate(h == 0, step))
            copy.start()
            near.append((h, index, step, copy))
    for h in range(2):
        forward(h, 0, part(h, 0))
    far = []
    for h, index, step, copy in near:
        copy.wait_recv()
        ref = part(h, 4 - step, index * (block // 2), block // 2)
        onward = remote(ref, ref, send.at[1, h, 2 + index], recv.at[1, h, 2 + index], mate(h == 0, step))
        onward.start()
        far.append(onward)
        forward(h, 1 + index, part(h, 4 - step))
        started.append(copy)
    for copy in far:
        copy.wait_recv()
    for h in range(2):
        forward(h, 3, part(h, 2))
    for copy in across:
        copy.wait_recv()
    for copy in started + far + across:
        copy.wait_send()


def order_of_z():
    steps = []
    for step in range(1, Z // 2 + 1):
        steps.append(step)
        if step != Z - step:
            steps.append(Z - step)
    return steps


class Regroup:
    def __init__(self, source, out, beside, landed, sems, spot):
        self.source, self.out, self.beside, self.landed = source, out, beside, landed
        self.p_send, self.p_recv, self.z_send, self.z_recv, self.y_send, self.y_recv, self.local = sems
        self.x, self.y, self.z, self.core = spot
        self.origin = (self.core, 1 - self.core)
        self.pair = remote(
            source.at[:, :, 1 - self.core], beside, self.p_send, self.p_recv,
            device(self.x, self.y, self.z, 1 - self.core),
        )
        self.done = []
        self.plane = []
        self.kept = []

    def leaving(self, path, z):
        return self.source.at[z, :, self.core] if path == 0 else self.beside.at[z]

    def landing(self, path, z):
        return self.landed.at[self.origin[path], z]

    def start_z(self, path):
        x, y, z, core = self.x, self.y, self.z, self.core
        if path == 1:
            self.pair.wait_recv()
        for step in order_of_z():
            target = lax.rem(z + step, Z)
            copy = remote(
                self.leaving(path, target), self.landing(path, z), self.z_send.at[path, step], self.z_recv.at[path, z],
                device(x, y, target, core),
            )
            copy.start()
            self.done.append(copy)
        pltpu.make_async_copy(self.leaving(path, z), self.landing(path, z), self.local.at[path]).start()

    def arrive(self, path, source):
        spot = self.landing(path, source)

        @pl.when(self.z != source)
        def _():
            remote(
                spot, spot, self.z_send.at[path, 0], self.z_recv.at[path, source],
                device(self.x, self.y, source, self.core),
            ).wait_recv()

        @pl.when(self.z == source)
        def _():
            pltpu.make_async_copy(spot, spot, self.local.at[path]).wait()

    def start_plane(self, path):
        x, y, z, core = self.x, self.y, self.z, self.core
        origin = self.origin[path]
        for turn, offset in enumerate((0, 1, 3, 2)):
            first = lax.rem(z // 4 + offset, 4) * 4
            for step in range(4):
                self.arrive(path, first + step)
            group = pl.ds(first, 4)
            landing = self.out.at[group, y, origin, x]
            for along_y in range(Y):
                for along_x in range(X):
                    if along_x or along_y:
                        to_x, to_y = lax.rem(x + along_x, X), lax.rem(y + along_y, Y)
                        index = along_y * X + along_x
                        copy = remote(
                            self.landed.at[origin, group, to_y, to_x], landing,
                            self.y_send.at[path, turn, index], self.y_recv.at[path, turn, index],
                            device(to_x, to_y, z, core),
                        )
                        copy.start()
                        self.plane.append(copy)
            keep = pltpu.make_async_copy(
                self.landed.at[origin, group, y, x], landing, self.local.at[2 + 4 * path + turn]
            )
            keep.start()
            self.kept.append(keep)

    def finish(self):
        for copy in self.plane:
            copy.wait_recv()
        for keep in self.kept:
            keep.wait()
        for copy in self.plane + self.done + [self.pair]:
            copy.wait_send()


def gather_part(orbitals, piece, slab, rows, across, beside, landed, moving, sems, spot):
    q_send, q_recv, send, recv = sems
    x, y, z, core = spot
    regroup = Regroup(orbitals, slab, beside, landed, moving, (x, y, z, core))
    regroup.pair.start()
    first = []
    for step in order_of_z():
        copy = remote(
            piece, rows.at[z, y, core, x], q_send.at[step], q_recv.at[step], device(x, y, lax.rem(z + step, Z), core)
        )
        copy.start()
        first.append(copy)
    regroup.start_z(0)
    regroup.start_z(1)
    rows[z, y, core, x] = piece[...]
    for copy in first:
        copy.wait_recv()
    second = []
    mine = rows.at[:, y, core, x]
    for step in range(1, Y):
        copy = remote(
            mine, mine, send.at[0, step], recv.at[0, step], device(x, lax.rem(y + step, Y), z, core)
        )
        copy.start()
        second.append(copy)
    for copy in second:
        copy.wait_recv()
    sibling = device(x, y, z, 1 - core)
    near, far, last = [], [], []

    def along_x(step):
        return device(lax.rem(x + step, X), y, z, core)

    def forward(index, ref):
        copy = remote(ref, ref, send.at[2, index], recv.at[2, index], sibling)
        copy.start()
        last.append(copy)

    mine = rows.at[:, :, core, x]
    for index, step in ((0, 1), (1, 3)):
        copy = remote(mine, mine, send.at[1, index], recv.at[1, index], along_x(step))
        copy.start()
        near.append(copy)
    forward(0, mine)
    for index, step in ((0, 1), (1, 3)):
        near[index].wait_recv()
        source = lax.rem(x + 4 - step, X)
        ref = rows.at[pl.ds(index * (Z // 2), Z // 2), :, core, source]
        copy = remote(ref, ref, send.at[1, 2 + index], recv.at[1, 2 + index], along_x(step))
        copy.start()
        far.append(copy)
        forward(1 + index, rows.at[:, :, core, source])
    regroup.start_plane(0)
    for copy in far:
        copy.wait_recv()
    forward(3, rows.at[:, :, core, lax.rem(x + 2, X)])
    for copy in last:
        copy.wait_recv()
    for part in range(BLOCKS):
        block = rows[2 * part:2 * part + 2].reshape(64, 16, 128).reshape(128, 8, 128).reshape(128, NB)
        across[:, part * BLOCK:(part + 1) * BLOCK] = block.T
    regroup.start_plane(1)
    regroup.finish()
    for copy in first + second + near + far + last:
        copy.wait_send()


def plane_part(landed, ordered, out, arrive, sems, spot):
    send, recv, kept = sems
    x, y, z, core = spot
    copies = []
    keeps = []
    for turn, offset in enumerate((0, 1, 3, 2)):
        first = lax.rem(z // 4 + offset, 4) * 4
        for step in range(4):
            arrive(first + step)
        group = pl.ds(first, 4)
        ordered[group] = landed[group].reshape(4, CORES, Y, X, 2, landed.shape[-1])
        landing = out.at[group, y, :, x]
        for along_y in range(Y):
            for along_x in range(X):
                if along_x or along_y:
                    to_x, to_y = lax.rem(x + along_x, X), lax.rem(y + along_y, Y)
                    index = along_y * X + along_x
                    copy = remote(
                        ordered.at[group, :, to_y, to_x], landing, send.at[turn, index], recv.at[turn, index],
                        device(to_x, to_y, z, core),
                    )
                    copy.start()
                    copies.append(copy)
        keep = pltpu.make_async_copy(ordered.at[group, :, y, x], landing, kept.at[turn])
        keep.start()
        keeps.append(keep)
    for copy in copies:
        copy.wait_recv()
    for copy in copies:
        copy.wait_send()
    for keep in keeps:
        keep.wait()


def gram_part(across, slab, products, out, theirs, terms, got0, got1, got2, got3, plane, summed, sems, spot):
    send, recv, r_send, r_recv, z_send, z_recv, g_send, g_recv, p_send, p_recv = sems
    x, y, z, core = spot
    pairs = []
    columns = slab[...].reshape(NB, slab.shape[-1])
    for part in range(4):
        rows = slice(part * 256, (part + 1) * 256)
        products[rows, :] = (dot(across[rows, :], columns) * (1.0 / math.sqrt(NB))).astype(jnp.bfloat16)
        pair = remote(
            products.at[rows, :], theirs.at[rows, :], p_send.at[part], p_recv.at[part], device(x, y, z, 1 - core)
        )
        pair.start()
        pairs.append(pair)
    contract = (((1,), (1,)), ((), ()))

    def add(source, again):
        for which in range(CORES):

            @pl.when(core == which)
            def _():
                count = 0
                for i in ROWS_OF_CORE[which]:
                    row = lax.dot_general(
                        source[i * BLOCK:(i + 1) * BLOCK, :], source[i * BLOCK:, :], contract,
                        preferred_element_type=jnp.float32,
                    )
                    for j in range(BLOCKS - i):
                        tiles = slice(count * 16, (count + 1) * 16)
                        term = row[:, j * BLOCK:(j + 1) * BLOCK].reshape(16, 8, 128)
                        terms[tiles] = terms[tiles] + term if again else term
                        count += 1

    add(products, False)
    for pair in pairs:
        pair.wait_recv()
    add(theirs, True)

    unit = OWNERS
    half = 16 * unit
    firsts = (x, y)
    seconds = (y, x)

    def mate(axis_is_x, step):
        if axis_is_x:
            return device(lax.rem(x + step, X), y, z, core)
        return device(x, lax.rem(y + step, Y), z, core)

    block = 4 * unit
    middle = block // 2

    def span(h, where, begin=0, size=block):
        return pl.ds(h * half + lax.rem(firsts[h] + where, 4) * block + begin, size)

    copies = []
    for h in range(2):
        for index, step in ((0, 1), (1, 3)):
            copy = remote(
                terms.at[span(h, 2, index * middle, middle)], got0.at[h, index],
                r_send.at[0, h, index], r_recv.at[0, h, index], mate(h == 0, step),
            )
            copy.start()
            copies.append((h, index, step, copy))
    near = []
    for h, index, step, copy in copies:
        copy.wait_recv()
        part = span(h, step, index * middle, middle)
        terms[part] = terms[part] + got0[h, index]
        onward = remote(
            terms.at[span(h, step)], got1.at[h, index], r_send.at[2, h, index], r_recv.at[2, h, index],
            mate(h == 0, step),
        )
        onward.start()
        near.append(onward)
    copies = [copy for _, _, _, copy in copies] + near
    for copy in near:
        copy.wait_recv()
    for h in range(2):
        mine = span(h, 0)
        terms[mine] = terms[mine] + (got1[h, 0] + got1[h, 1])
    later = []
    for step in range(1, 4):
        for h in range(2):
            target = lax.rem(seconds[h] + step, 4)
            copy = remote(
                terms.at[pl.ds(h * half + (firsts[h] * 4 + target) * unit, unit)],
                got2.at[h, step - 1],
                r_send.at[1, h, step],
                r_recv.at[1, h, step],
                mate(h == 1, step),
            )
            copy.start()
            later.append(copy)
    for copy in later:
        copy.wait_recv()
    starts = [h * half + (firsts[h] * 4 + seconds[h]) * unit for h in range(2)]
    for h in range(2):
        mine = pl.ds(starts[h], unit)
        plane[:, h] = terms[mine] + (got2[h, 0] + got2[h, 1]) + got2[h, 2]

    def to_owner(step):
        target = lax.rem(z + step, Z)
        tile = jnp.minimum(target, OWNERS - 1)
        return target, remote(
            plane.at[tile], got3.at[step - 1], z_send.at[step], z_recv.at[step], device(x, y, target, core)
        )

    for step in order_of_z():
        target, copy = to_owner(step)

        @pl.when(target < OWNERS)
        def _():
            copy.start()

    tile = jnp.minimum(z, OWNERS - 1)

    def to_all(step):
        return remote(
            summed.at[tile], summed.at[tile], g_send.at[step], g_recv.at[step],
            device(x, y, lax.rem(z + step, Z), core),
        )

    @pl.when(z < OWNERS)
    def _():
        for step in order_of_z():
            to_owner(step)[1].wait_recv()
        total = plane[tile]
        for step in range(1, Z):
            total = total + got3[step - 1]
        summed[tile] = total
        for step in order_of_z():
            to_all(step).start()

    for step in order_of_z():
        source = lax.rem(z + Z - step, Z)

        @pl.when(source < OWNERS)
        def _():
            to_all(step).wait_recv()

    for h in range(2):
        out[pl.ds(core * 2 * half + starts[h], unit)] = summed[:, h]
    spread(out, unit, x, y, z, core, send, recv)

    for step in range(1, Z):
        target, copy = to_owner(step)

        @pl.when(target < OWNERS)
        def _():
            copy.wait_send()

    @pl.when(z < OWNERS)
    def _():
        for step in range(1, Z):
            to_all(step).wait_send()

    for copy in copies + later + pairs:
        copy.wait_send()


def split(value):
    high = value.astype(jnp.bfloat16)
    return high, (value - high.astype(jnp.float32)).astype(jnp.bfloat16)


def dot(a, b):
    return jnp.dot(a, b, preferred_element_type=jnp.float32)


def factor_block(load, lane, row):
    full = (8, 128)
    groups = [load(g) for g in range(16)]
    for quarter in range(4):
        first = 4 * quarter
        for g in range(first, first + 4):
            at = 8 * g
            panel = groups[g]
            columns = [jnp.broadcast_to(panel[:, at + t:at + t + 1], full) for t in range(8)]
            a = [[jnp.broadcast_to(columns[t][i:i + 1, :], full) for t in range(i + 1)] for i in range(8)]
            below = [[None] * 8 for _ in range(8)]
            scale = []
            for s in range(8):
                r = lax.rsqrt(a[s][s])
                scale.append(r)
                for i in range(s + 1, 8):
                    below[i][s] = a[i][s] * r
                for i in range(s + 1, 8):
                    for t in range(s + 1, i + 1):
                        a[i][t] = a[i][t] - below[i][s] * below[t][s]
            inside = (lane >= at) & (lane < at + 8)
            panel = jnp.where(inside, (lane == row + at).astype(jnp.float32), panel)
            solved = []
            for s in range(8):
                value = jnp.broadcast_to(panel[s:s + 1, :], full)
                for t in range(s):
                    value = value - below[s][t] * solved[t]
                solved.append(value * scale[s])
            result = solved[0]
            for s in range(1, 8):
                result = jnp.where(row == s, solved[s], result)
            groups[g] = result
            for other in range(g + 1, first + 4):
                target = groups[other]
                left = []
                for s in range(8):
                    value = jnp.broadcast_to(target[:, at + s:at + s + 1], full)
                    for t in range(s):
                        value = value - below[s][t] * left[t]
                    left.append(value * scale[s])
                target = jnp.where(inside, 0.0, target)
                for s in range(8):
                    target = target - left[s] * solved[s]
                groups[other] = target
        if quarter < 3:
            at = 32 * quarter
            inside = (lane >= at) & (lane < at + 32)
            rows = jnp.concatenate(
                [
                    jnp.where(inside & (lane > 8 * g + row), 0.0, groups[g])
                    for g in range(first, first + 4)
                ],
                axis=0,
            )
            turned = rows.T[at + 32:, :]
            high, low = split(rows)
            turned_high, turned_low = split(turned)
            change = dot(turned_high, high) + dot(turned_low, high) + dot(turned_high, low)
            for other in range(first + 4, 16):
                begin = (other - first - 4) * 8
                groups[other] = jnp.where(inside, 0.0, groups[other]) - change[begin:begin + 8, :]
    return [jnp.where(lane > 8 * g + row, 0.0, groups[g]) for g in range(16)]


class Leave:
    def __init__(self, ready, beside, landed, sems, spot):
        self.ready, self.beside, self.landed = ready, beside, landed
        self.p_send, self.p_recv, self.z_send, self.z_recv, self.local = sems
        self.x, self.y, self.z, self.core = spot

    def pair(self, k):
        return remote(
            self.ready.at[k, 1 - self.core], self.beside.at[k], self.p_send.at[k], self.p_recv.at[k],
            device(self.x, self.y, self.z, 1 - self.core),
        )

    def source(self, path, k, part):
        return self.ready.at[k, self.core, part] if path == 0 else self.beside.at[k, part]

    def origin(self, path):
        return self.core if path == 0 else 1 - self.core

    def along(self, path, k, part):
        return remote(
            self.source(path, k, part), self.landed.at[self.z, self.origin(path)],
            self.z_send.at[path, 2 * k + part], self.z_recv.at[path, self.z],
            device(self.x, self.y, 2 * k + part, self.core),
        )

    def keep(self, path, k, part):
        return pltpu.make_async_copy(
            self.source(path, k, part), self.landed.at[self.z, self.origin(path)], self.local.at[path]
        )

    def start(self, path, k):
        if path == 1:
            self.pair(k).wait_recv()
        for part in range(2):

            @pl.when(self.z != 2 * k + part)
            def _():
                self.along(path, k, part).start()

            @pl.when(self.z == 2 * k + part)
            def _():
                self.keep(path, k, part).start()

    def arrive(self, source):
        @pl.when(self.z != source)
        def _():
            for path in range(2):
                spot = self.landed.at[source, self.origin(path)]
                remote(
                    spot, spot, self.z_send.at[path, source], self.z_recv.at[path, source],
                    device(self.x, self.y, source, self.core),
                ).wait_recv()

        @pl.when(self.z == source)
        def _():
            for path in range(2):
                spot = self.landed.at[source, self.origin(path)]
                pltpu.make_async_copy(spot, spot, self.local.at[path]).wait()

    def finish(self):
        for path in range(2):
            for k in range(BLOCKS):
                for part in range(2):

                    @pl.when(self.z != 2 * k + part)
                    def _():
                        self.along(path, k, part).wait_send()

        for k in range(BLOCKS):
            self.pair(k).wait_send()


def solve(gram, products, mat, leave):
    ready = leave.ready
    lane = lax.broadcasted_iota(jnp.int32, (8, 128), 1)
    row = lax.broadcasted_iota(jnp.int32, (8, 128), 0)
    count = 0
    for rows in ROWS_OF_CORE:
        for i in rows:
            for j in range(i, BLOCKS):
                mat[i * BLOCK:(i + 1) * BLOCK, j * BLOCK:(j + 1) * BLOCK] = (
                    gram[count * 16:(count + 1) * 16].reshape(BLOCK, BLOCK) * (1.0 / 131072.0)
                )
                count += 1
            if i:
                mat[i * BLOCK:(i + 1) * BLOCK, :i * BLOCK] = jnp.zeros((BLOCK, i * BLOCK), jnp.float32)

    first = mat[:BLOCK, :BLOCK]
    own = jnp.concatenate(factor_block(lambda g: first[8 * g:8 * g + 8, :], lane, row), axis=0)
    for k in range(BLOCKS):
        at = k * BLOCK
        after = at + BLOCK
        here = slice(at, after)
        mat[here, here] = own
        high, low = split(own)
        left = jnp.concatenate([high, low], axis=1)
        for start, stop in ((0, at), (after, NB)):
            if start < stop:
                up, down = split(mat[here, start:stop])
                mat[here, start:stop] = dot(left, jnp.concatenate([up, up], axis=0)) + dot(high, down)
        if after < NB:
            turned_high, turned_low = split(mat[here, after:].T)
            turned = jnp.concatenate([turned_high, turned_low], axis=1)

            def change(begin, end, start, stop):
                rows = slice(begin - after, end - after)
                up, down = split(mat[here, start:stop])
                return dot(turned[rows], jnp.concatenate([up, up], axis=0)) + dot(turned_high[rows], down)

            following = slice(after, after + BLOCK)
            corner = mat[following, following] - change(after, after + BLOCK, after, after + BLOCK)
            own = jnp.concatenate(factor_block(lambda g: corner[8 * g:8 * g + 8, :], lane, row), axis=0)
            mat[after:, here] = -change(after, NB, at, after)
            for start in range(0, at, 256):
                stop = min(start + 256, at)
                mat[after:, start:stop] = mat[after:, start:stop] - change(after, NB, start, stop)
            for start in range(after, NB, 256):
                stop = min(start + 256, NB)
                mat[after:stop, start:stop] = mat[after:stop, start:stop] - change(after, stop, start, stop)
        inverse = jnp.concatenate(
            [
                mat[at + 64 * to_z + 16 * to_y + 8 * to_core:at + 64 * to_z + 16 * to_y + 8 * to_core + 8, :after]
                for to_core in range(CORES)
                for to_z in range(2)
                for to_y in range(Y)
            ],
            axis=0,
        ).astype(jnp.bfloat16)
        local = dot(inverse, products[:after, :]).astype(jnp.bfloat16)
        for to_core in range(CORES):
            for to_z in range(2):
                begin = 64 * to_core + 32 * to_z
                ready[k, to_core, to_z] = local[begin:begin + 32, :]
        leave.pair(k).start()
        leave.start(0, k)
        if k:
            leave.start(1, k - 1)
    leave.start(1, BLOCKS - 1)


def whole_kernel(orbitals, piece, out, *scratch):
    buffers, sems = scratch[:BUFFERS], scratch[BUFFERS:]
    (
        beside, landed, slab, rows, across, products, gram, theirs, terms, got0, got1, got2, got3,
        plane, summed, mat, ready, beside2, landed2, ordered,
    ) = buffers
    spot = place()
    greet(*spot, True)
    gather_part(orbitals, piece, slab, rows, across, beside, landed, sems[:7], sems[7:11], spot)
    gram_part(across, slab, products, gram, theirs, terms, got0, got1, got2, got3, plane, summed, sems[11:21], spot)
    leave = Leave(ready, beside2, landed2, sems[21:26], spot)
    solve(gram, products, mat, leave)
    plane_part(landed2, ordered, out, leave.arrive, sems[26:29], spot)
    leave.finish()


BUFFERS = 20


def whole(orbitals, piece):
    points = orbitals.shape[-1]
    unit = OWNERS
    dma = pltpu.SemaphoreType.DMA
    narrow, wide = jnp.bfloat16, jnp.float32
    entries = (Z, Y, CORES, X, 2, points)
    held = Y * X * 2
    buffers = [
        pltpu.VMEM((Z, Y, X, 2, points), narrow),
        pltpu.VMEM((CORES, Z, Y, X, 2, points), narrow),
        pltpu.VMEM(entries, narrow),
        pltpu.VMEM((Z, Y, CORES, X, 16, 128), narrow),
        pltpu.VMEM((NB, NB), narrow),
        pltpu.VMEM((NB, points), narrow),
        pltpu.VMEM((TILES, 8, 128), wide),
        pltpu.VMEM((NB, points), narrow),
        pltpu.VMEM((TILES // 2, 8, 128), wide),
        pltpu.VMEM((2, 2, 2 * unit, 8, 128), wide),
        pltpu.VMEM((2, 2, 4 * unit, 8, 128), wide),
        pltpu.VMEM((2, 3, unit, 8, 128), wide),
        pltpu.VMEM((Z - 1, 2, 8, 128), wide),
        pltpu.VMEM((OWNERS, 2, 8, 128), wide),
        pltpu.VMEM((OWNERS, 2, 8, 128), wide),
        pltpu.VMEM((NB, NB), wide),
        pltpu.VMEM((BLOCKS, CORES, 2, held, points), narrow),
        pltpu.VMEM((BLOCKS, 2, held, points), narrow),
        pltpu.VMEM((Z, CORES, held, points), narrow),
        pltpu.VMEM((Z, CORES, Y, X, 2, points), narrow),
    ]
    sems = [
        dma, dma, dma((2, Z)), dma((2, Z)), dma((2, 4, X * Y)), dma((2, 4, X * Y)), dma((10,)),
        dma((Z,)), dma((Z,)), dma((3, 4)), dma((3, 4)),
        dma((3, 2, 4)), dma((3, 2, 4)), dma((3, 2, 4)), dma((3, 2, 4)),
        dma((Z,)), dma((Z,)), dma((Z,)), dma((Z,)), dma((4,)), dma((4,)),
        dma((BLOCKS,)), dma((BLOCKS,)), dma((2, Z)), dma((2, Z)), dma((2,)),
        dma((4, X * Y)), dma((4, X * Y)), dma((4,)),
    ]
    return pl.pallas_call(
        whole_kernel,
        out_shape=jax.ShapeDtypeStruct(entries, narrow),
        in_specs=[pl.BlockSpec(memory_space=pltpu.VMEM)] * 2,
        out_specs=pl.BlockSpec(memory_space=pltpu.VMEM),
        scratch_shapes=buffers + sems,
        compiler_params=pltpu.CompilerParams(collective_id=0, has_side_effects=True, vmem_limit_bytes=VMEM),
        name="localize",
    )(orbitals, piece)


def pick(orbitals, pivots):
    folded = orbitals.reshape(2, 1024, 128)
    outer = (pivots[:, None] // 128 == jnp.arange(1024, dtype=jnp.int32)[None, :]).astype(jnp.bfloat16)
    inner = pivots[:, None] % 128 == jnp.arange(128, dtype=jnp.int32)[None, :]
    rows = jnp.einsum("jh,rhl->rjl", outer, folded, preferred_element_type=jnp.float32)
    return jnp.sum(jnp.where(inner[None], rows, 0.0), axis=2).astype(jnp.bfloat16)


def body(orbitals, pivots):
    points = orbitals.shape[1] // 512
    entries = (Z, Y, CORES, X, 2, points)
    piece = pick(orbitals, pivots).reshape(16, 128)
    outgoing = orbitals.reshape(2, 512, points).transpose(1, 0, 2).reshape(entries)
    returned = whole(outgoing, piece)
    return returned.reshape(512, 2, points).transpose(1, 0, 2).reshape(orbitals.shape)


def solution(mesh):
    placed = (P(("grid", "band"), None), P())
    return jax.shard_map(
        body, mesh=mesh, in_specs=placed, out_specs=P(("grid", "band"), None), check_vma=False
    )
```

```python
import functools
import math

import jax
import jax.numpy as jnp
from jax import lax
from jax.experimental import pallas as pl
from jax.experimental.pallas import tpu as pltpu
from jax.sharding import PartitionSpec as P

MESH = pl.DeviceIdType.MESH
X, Y, Z, CORES = 4, 4, 16, 2
NB = 1024
BLOCK = 128
BLOCKS = NB // BLOCK
TILES = 576
UNITS = (5, 4)
OWNERS = (0, 8)
ROWS_OF_CORE = ((0, 3, 4, 7), (1, 2, 5, 6))
VMEM = 48 * 1024 * 1024


def place():
    grid = lax.axis_index("grid")
    return lax.axis_index("band"), lax.rem(grid // CORES, Y), grid // (CORES * Y), lax.rem(grid, CORES)


def device(x, y, z, core):
    return ((z * Y + y) * CORES + core, x)


def greet(x, y, z, core, plane):
    barrier = pltpu.get_barrier_semaphore()
    partners = [device(x, y, z, 1 - core)]
    for along_y in range(Y):
        for along_x in range(X):
            if (along_x or along_y) and (plane or not (along_x and along_y)):
                partners.append(device(lax.rem(x + along_x, X), lax.rem(y + along_y, Y), z, core))
    for step in range(1, Z):
        partners.append(device(x, y, lax.rem(z + step, Z), core))
    for partner in partners:
        pl.semaphore_signal(barrier, inc=1, device_id=partner, device_id_type=MESH)
    pl.semaphore_wait(barrier, len(partners))


def remote(src, dst, send, recv, target):
    return pltpu.make_async_remote_copy(
        src_ref=src, dst_ref=dst, send_sem=send, recv_sem=recv, device_id=target, device_id_type=MESH
    )


def order_of_z():
    steps = []
    for step in range(1, Z // 2 + 1):
        steps.append(step)
        if step != Z - step:
            steps.append(Z - step)
    return steps


class Regroup:
    def __init__(self, source, out, beside, landed, sems, spot):
        self.source, self.out, self.beside, self.landed = source, out, beside, landed
        self.p_send, self.p_recv, self.z_send, self.z_recv, self.y_send, self.y_recv, self.local = sems
        self.x, self.y, self.z, self.core = spot
        self.origin = (self.core, 1 - self.core)
        self.pair = remote(
            source.at[:, :, 1 - self.core], beside, self.p_send, self.p_recv,
            device(self.x, self.y, self.z, 1 - self.core),
        )
        self.done = []
        self.plane = []
        self.kept = []

    def leaving(self, path, z):
        return self.source.at[z, :, self.core] if path == 0 else self.beside.at[z]

    def landing(self, path, z):
        return self.landed.at[self.origin[path], z]

    def start_z(self, path):
        x, y, z, core = self.x, self.y, self.z, self.core
        if path == 1:
            self.pair.wait_recv()
        for step in order_of_z():
            target = lax.rem(z + step, Z)
            copy = remote(
                self.leaving(path, target), self.landing(path, z), self.z_send.at[path, step], self.z_recv.at[path, z],
                device(x, y, target, core),
            )
            copy.start()
            self.done.append(copy)
        pltpu.make_async_copy(self.leaving(path, z), self.landing(path, z), self.local.at[path]).start()

    def arrive(self, path, source):
        spot = self.landing(path, source)

        @pl.when(self.z != source)
        def _():
            remote(
                spot, spot, self.z_send.at[path, 0], self.z_recv.at[path, source],
                device(self.x, self.y, source, self.core),
            ).wait_recv()

        @pl.when(self.z == source)
        def _():
            pltpu.make_async_copy(spot, spot, self.local.at[path]).wait()

    def start_plane(self, path):
        x, y, z, core = self.x, self.y, self.z, self.core
        origin = self.origin[path]
        for turn, offset in enumerate((0, 1, 3, 2)):
            first = lax.rem(z // 4 + offset, 4) * 4
            for step in range(4):
                self.arrive(path, first + step)
            group = pl.ds(first, 4)
            landing = self.out.at[group, y, origin, x]
            for along_y in range(Y):
                for along_x in range(X):
                    if along_x or along_y:
                        to_x, to_y = lax.rem(x + along_x, X), lax.rem(y + along_y, Y)
                        index = along_y * X + along_x
                        copy = remote(
                            self.landed.at[origin, group, to_y, to_x], landing,
                            self.y_send.at[path, turn, index], self.y_recv.at[path, turn, index],
                            device(to_x, to_y, z, core),
                        )
                        copy.start()
                        self.plane.append(copy)
            keep = pltpu.make_async_copy(
                self.landed.at[origin, group, y, x], landing, self.local.at[2 + 4 * path + turn]
            )
            keep.start()
            self.kept.append(keep)

    def finish(self):
        for copy in self.plane:
            copy.wait_recv()
        for keep in self.kept:
            keep.wait()
        for copy in self.plane + self.done + [self.pair]:
            copy.wait_send()


def gather_part(orbitals, piece, slab, rows, across, beside, landed, moving, sems, spot):
    q_send, q_recv, send, recv = sems
    x, y, z, core = spot
    regroup = Regroup(orbitals, slab, beside, landed, moving, (x, y, z, core))
    regroup.pair.start()
    first = []
    for step in order_of_z():
        copy = remote(
            piece, rows.at[z, y, core, x], q_send.at[step], q_recv.at[step], device(x, y, lax.rem(z + step, Z), core)
        )
        copy.start()
        first.append(copy)
    regroup.start_z(0)
    regroup.start_z(1)
    rows[z, y, core, x] = piece[...]
    for copy in first:
        copy.wait_recv()
    second = []
    mine = rows.at[:, y, core, x]
    for step in range(1, Y):
        copy = remote(
            mine, mine, send.at[0, step], recv.at[0, step], device(x, lax.rem(y + step, Y), z, core)
        )
        copy.start()
        second.append(copy)
    for copy in second:
        copy.wait_recv()
    sibling = device(x, y, z, 1 - core)
    near, far, last = [], [], []

    def along_x(step):
        return device(lax.rem(x + step, X), y, z, core)

    def forward(index, ref):
        copy = remote(ref, ref, send.at[2, index], recv.at[2, index], sibling)
        copy.start()
        last.append(copy)

    mine = rows.at[:, :, core, x]
    for index, step in ((0, 1), (1, 3)):
        copy = remote(mine, mine, send.at[1, index], recv.at[1, index], along_x(step))
        copy.start()
        near.append(copy)
    forward(0, mine)
    for index, step in ((0, 1), (1, 3)):
        near[index].wait_recv()
        source = lax.rem(x + 4 - step, X)
        ref = rows.at[pl.ds(index * (Z // 2), Z // 2), :, core, source]
        copy = remote(ref, ref, send.at[1, 2 + index], recv.at[1, 2 + index], along_x(step))
        copy.start()
        far.append(copy)
        forward(1 + index, rows.at[:, :, core, source])
    regroup.start_plane(0)
    for copy in far:
        copy.wait_recv()
    forward(3, rows.at[:, :, core, lax.rem(x + 2, X)])
    for copy in last:
        copy.wait_recv()
    for part in range(BLOCKS):
        block = rows[2 * part:2 * part + 2].reshape(64, 16, 128).reshape(128, 8, 128).reshape(128, NB)
        across[:, part * BLOCK:(part + 1) * BLOCK] = block.T
    regroup.start_plane(1)
    regroup.finish()
    for copy in first + second + near + far + last:
        copy.wait_send()


def plane_part(landed, ordered, out, arrive, sems, spot):
    send, recv, kept = sems
    x, y, z, core = spot
    copies = []
    keeps = []
    for turn, offset in enumerate((0, 1, 3, 2)):
        first = lax.rem(z // 4 + offset, 4) * 4
        for step in range(4):
            arrive(first + step)
        group = pl.ds(first, 4)
        ordered[group] = landed[group].reshape(4, CORES, Y, X, 2, landed.shape[-1])
        landing = out.at[group, y, :, x]
        for along_y in range(Y):
            for along_x in range(X):
                if along_x or along_y:
                    to_x, to_y = lax.rem(x + along_x, X), lax.rem(y + along_y, Y)
                    index = along_y * X + along_x
                    copy = remote(
                        ordered.at[group, :, to_y, to_x], landing, send.at[turn, index], recv.at[turn, index],
                        device(to_x, to_y, z, core),
                    )
                    copy.start()
                    copies.append(copy)
        keep = pltpu.make_async_copy(ordered.at[group, :, y, x], landing, kept.at[turn])
        keep.start()
        keeps.append(keep)
    for copy in copies:
        copy.wait_recv()
    for copy in copies:
        copy.wait_send()
    for keep in keeps:
        keep.wait()


def sum_wave(wave, out, terms, buffers, sems, spot):
    got0, got1, got2, got3, plane, summed = buffers
    send, recv, r_send, r_recv, z_send, z_recv, g_send, g_recv = sems
    x, y, z, core = spot
    unit = UNITS[wave]
    first_owner = OWNERS[wave]
    half = 16 * unit
    block = 4 * unit
    middle = block // 2
    begin = sum(UNITS[:wave]) * 32
    goal = core * (TILES // 2) + begin
    firsts = (x, y)
    seconds = (y, x)
    sent = []

    def mate(axis_is_x, step):
        if axis_is_x:
            return device(lax.rem(x + step, X), y, z, core)
        return device(x, lax.rem(y + step, Y), z, core)

    def span(base, h, where, start=0, size=block):
        return pl.ds(base + h * half + lax.rem(firsts[h] + where, 4) * block + start, size)

    def launch(*args):
        copy = remote(*args)
        copy.start()
        sent.append(copy)
        return copy

    far = [
        (h, index, step, launch(
            terms.at[span(begin, h, 2, index * middle, middle)], got0.at[h, index],
            r_send.at[wave, 0, h, index], r_recv.at[wave, 0, h, index], mate(h == 0, step),
        ))
        for h in range(2) for index, step in ((0, 1), (1, 3))
    ]
    yield
    near = []
    for h, index, step, copy in far:
        copy.wait_recv()
        part = span(begin, h, step, index * middle, middle)
        terms[part] = terms[part] + got0[h, index]
        near.append(launch(
            terms.at[span(begin, h, step)], got1.at[h, index], r_send.at[wave, 2, h, index],
            r_recv.at[wave, 2, h, index], mate(h == 0, step),
        ))
    yield
    for copy in near:
        copy.wait_recv()
    later = []
    for h in range(2):
        mine = span(begin, h, 0)
        terms[mine] = terms[mine] + (got1[h, 0] + got1[h, 1])
    for step in range(1, 4):
        for h in range(2):
            target = lax.rem(seconds[h] + step, 4)
            later.append(launch(
                terms.at[pl.ds(begin + h * half + (firsts[h] * 4 + target) * unit, unit)], got2.at[h, step - 1],
                r_send.at[wave, 1, h, step], r_recv.at[wave, 1, h, step], mate(h == 1, step),
            ))
    yield
    for copy in later:
        copy.wait_recv()
    starts = [h * half + (firsts[h] * 4 + seconds[h]) * unit for h in range(2)]
    for h in range(2):
        mine = pl.ds(begin + starts[h], unit)
        plane[:, h] = terms[mine] + (got2[h, 0] + got2[h, 1]) + got2[h, 2]

    def owns(where):
        return (where >= first_owner) & (where < first_owner + unit)

    def tile_of(where):
        return jnp.clip(where - first_owner, 0, unit - 1)

    def to_owner(step):
        target = lax.rem(z + step, Z)
        return target, remote(
            plane.at[tile_of(target)], got3.at[step - 1], z_send.at[wave, step], z_recv.at[wave, step],
            device(x, y, target, core),
        )

    for step in order_of_z():
        target, copy = to_owner(step)

        @pl.when(owns(target))
        def _():
            copy.start()

    yield
    tile = tile_of(z)

    def to_all(step, which):
        return remote(
            summed.at[which], summed.at[which], g_send.at[wave, step], g_recv.at[wave, step],
            device(x, y, lax.rem(z + step, Z), core),
        )

    @pl.when(owns(z))
    def _():
        for step in order_of_z():
            to_owner(step)[1].wait_recv()
        total = plane[tile]
        for step in range(1, Z):
            total = total + got3[step - 1]
        summed[tile] = total
        for step in order_of_z():
            to_all(step, tile).start()

    yield
    for step in order_of_z():
        source = lax.rem(z + Z - step, Z)

        @pl.when(owns(source))
        def _():
            to_all(step, tile_of(source)).wait_recv()

    inner = []
    for h in range(2):
        own = pl.ds(goal + starts[h], unit)
        out[own] = summed[:, h]
        for step in range(1, 4):
            inner.append(launch(
                out.at[own], out.at[own], send.at[wave, 0, h, step], recv.at[wave, 0, h, step], mate(h == 1, step)
            ))
    yield
    for copy in inner:
        copy.wait_recv()
    across = []

    def forward(h, index, ref):
        across.append(launch(
            ref, ref, send.at[wave, 2, h, index], recv.at[wave, 2, h, index], device(x, y, z, 1 - core)
        ))

    near = []
    for h in range(2):
        ref = out.at[span(goal, h, 0)]
        for index, step in ((0, 1), (1, 3)):
            near.append((h, index, step, launch(
                ref, ref, send.at[wave, 1, h, index], recv.at[wave, 1, h, index], mate(h == 0, step)
            )))
    for h in range(2):
        forward(h, 0, out.at[span(goal, h, 0)])
    yield
    far = []
    for h, index, step, copy in near:
        copy.wait_recv()
        ref = out.at[span(goal, h, 4 - step, index * middle, middle)]
        far.append(launch(
            ref, ref, send.at[wave, 1, h, 2 + index], recv.at[wave, 1, h, 2 + index], mate(h == 0, step)
        ))
        forward(h, 1 + index, out.at[span(goal, h, 4 - step)])
    yield
    for copy in far:
        copy.wait_recv()
    for h in range(2):
        forward(h, 3, out.at[span(goal, h, 2)])
    yield
    for copy in across:
        copy.wait_recv()
    yield
    for copy in sent:
        copy.wait_send()
    for step in range(1, Z):
        target, copy = to_owner(step)

        @pl.when(owns(target))
        def _():
            copy.wait_send()

    @pl.when(owns(z))
    def _():
        for step in range(1, Z):
            to_all(step, tile).wait_send()


def gram_part(across, slab, products, out, theirs, terms, buffers, sems, spot):
    p_send, p_recv = sems[-2:]
    x, y, z, core = spot
    pairs = []
    columns = slab[...].reshape(NB, slab.shape[-1])
    for part in range(4):
        rows = slice(part * 256, (part + 1) * 256)
        products[rows, :] = (dot(across[rows, :], columns) * (1.0 / math.sqrt(NB))).astype(jnp.bfloat16)
        pair = remote(
            products.at[rows, :], theirs.at[rows, :], p_send.at[part], p_recv.at[part], device(x, y, z, 1 - core)
        )
        pair.start()
        pairs.append(pair)
    contract = (((1,), (1,)), ((), ()))

    def add(source, again, begin, end):
        for which in range(CORES):

            @pl.when(core == which)
            def _():
                count = sum(BLOCKS - i for i in ROWS_OF_CORE[which][:begin])
                for i in ROWS_OF_CORE[which][begin:end]:
                    row = lax.dot_general(
                        source[i * BLOCK:(i + 1) * BLOCK, :], source[i * BLOCK:, :], contract,
                        preferred_element_type=jnp.float32,
                    )
                    for j in range(BLOCKS - i):
                        tiles = slice(count * 16, (count + 1) * 16)
                        term = row[:, j * BLOCK:(j + 1) * BLOCK].reshape(16, 8, 128)
                        terms[tiles] = terms[tiles] + term if again else term
                        count += 1

    add(products, False, 0, 4)
    for pair in pairs:
        pair.wait_recv()
    add(theirs, True, 0, 2)
    waves = [sum_wave(wave, out, terms, buffers[6 * wave:6 * wave + 6], sems[:-2], spot) for wave in range(2)]
    next(waves[0])
    add(theirs, True, 2, 4)
    next(waves[1])
    while waves:
        waves = [wave for wave in waves if next(wave, waves) is None]
    for pair in pairs:
        pair.wait_send()


def split(value):
    high = value.astype(jnp.bfloat16)
    return high, (value - high.astype(jnp.float32)).astype(jnp.bfloat16)


def dot(a, b):
    return jnp.dot(a, b, preferred_element_type=jnp.float32)


def factor_block(load, lane, row):
    full = (8, 128)
    groups = [load(g) for g in range(16)]
    for quarter in range(4):
        first = 4 * quarter
        for g in range(first, first + 4):
            at = 8 * g
            panel = groups[g]
            columns = [jnp.broadcast_to(panel[:, at + t:at + t + 1], full) for t in range(8)]
            a = [[jnp.broadcast_to(columns[t][i:i + 1, :], full) for t in range(i + 1)] for i in range(8)]
            below = [[None] * 8 for _ in range(8)]
            scale = []
            for s in range(8):
                r = lax.rsqrt(a[s][s])
                scale.append(r)
                for i in range(s + 1, 8):
                    below[i][s] = a[i][s] * r
                for i in range(s + 1, 8):
                    for t in range(s + 1, i + 1):
                        a[i][t] = a[i][t] - below[i][s] * below[t][s]
            inside = (lane >= at) & (lane < at + 8)
            panel = jnp.where(inside, (lane == row + at).astype(jnp.float32), panel)
            solved = []
            for s in range(8):
                value = jnp.broadcast_to(panel[s:s + 1, :], full)
                for t in range(s):
                    value = value - below[s][t] * solved[t]
                solved.append(value * scale[s])
            result = solved[0]
            for s in range(1, 8):
                result = jnp.where(row == s, solved[s], result)
            groups[g] = result
            for other in range(g + 1, first + 4):
                target = groups[other]
                left = []
                for s in range(8):
                    value = jnp.broadcast_to(target[:, at + s:at + s + 1], full)
                    for t in range(s):
                        value = value - below[s][t] * left[t]
                    left.append(value * scale[s])
                target = jnp.where(inside, 0.0, target)
                for s in range(8):
                    target = target - left[s] * solved[s]
                groups[other] = target
        if quarter < 3:
            at = 32 * quarter
            inside = (lane >= at) & (lane < at + 32)
            rows = jnp.concatenate(
                [
                    jnp.where(inside & (lane > 8 * g + row), 0.0, groups[g])
                    for g in range(first, first + 4)
                ],
                axis=0,
            )
            turned = rows.T[at + 32:, :]
            high, low = split(rows)
            turned_high, turned_low = split(turned)
            change = dot(turned_high, high) + dot(turned_low, high) + dot(turned_high, low)
            for other in range(first + 4, 16):
                begin = (other - first - 4) * 8
                groups[other] = jnp.where(inside, 0.0, groups[other]) - change[begin:begin + 8, :]
    return [jnp.where(lane > 8 * g + row, 0.0, groups[g]) for g in range(16)]


class Leave:
    def __init__(self, ready, beside, landed, sems, spot):
        self.ready, self.beside, self.landed = ready, beside, landed
        self.p_send, self.p_recv, self.z_send, self.z_recv, self.local = sems
        self.x, self.y, self.z, self.core = spot

    def pair(self, k):
        return remote(
            self.ready.at[k, 1 - self.core], self.beside.at[k], self.p_send.at[k], self.p_recv.at[k],
            device(self.x, self.y, self.z, 1 - self.core),
        )

    def source(self, path, k, part):
        return self.ready.at[k, self.core, part] if path == 0 else self.beside.at[k, part]

    def origin(self, path):
        return self.core if path == 0 else 1 - self.core

    def along(self, path, k, part):
        return remote(
            self.source(path, k, part), self.landed.at[self.z, self.origin(path)],
            self.z_send.at[path, 2 * k + part], self.z_recv.at[path, self.z],
            device(self.x, self.y, 2 * k + part, self.core),
        )

    def keep(self, path, k, part):
        return pltpu.make_async_copy(
            self.source(path, k, part), self.landed.at[self.z, self.origin(path)], self.local.at[path]
        )

    def start(self, path, k):
        if path == 1:
            self.pair(k).wait_recv()
        for part in range(2):

            @pl.when(self.z != 2 * k + part)
            def _():
                self.along(path, k, part).start()

            @pl.when(self.z == 2 * k + part)
            def _():
                self.keep(path, k, part).start()

    def arrive(self, source):
        @pl.when(self.z != source)
        def _():
            for path in range(2):
                spot = self.landed.at[source, self.origin(path)]
                remote(
                    spot, spot, self.z_send.at[path, source], self.z_recv.at[path, source],
                    device(self.x, self.y, source, self.core),
                ).wait_recv()

        @pl.when(self.z == source)
        def _():
            for path in range(2):
                spot = self.landed.at[source, self.origin(path)]
                pltpu.make_async_copy(spot, spot, self.local.at[path]).wait()

    def finish(self):
        for path in range(2):
            for k in range(BLOCKS):
                for part in range(2):

                    @pl.when(self.z != 2 * k + part)
                    def _():
                        self.along(path, k, part).wait_send()

        for k in range(BLOCKS):
            self.pair(k).wait_send()


def solve(gram, products, mat, leave):
    ready = leave.ready
    lane = lax.broadcasted_iota(jnp.int32, (8, 128), 1)
    row = lax.broadcasted_iota(jnp.int32, (8, 128), 0)
    count = 0
    for rows in ROWS_OF_CORE:
        for i in rows:
            for j in range(i, BLOCKS):
                mat[i * BLOCK:(i + 1) * BLOCK, j * BLOCK:(j + 1) * BLOCK] = (
                    gram[count * 16:(count + 1) * 16].reshape(BLOCK, BLOCK) * (1.0 / 131072.0)
                )
                count += 1
            if i:
                mat[i * BLOCK:(i + 1) * BLOCK, :i * BLOCK] = jnp.zeros((BLOCK, i * BLOCK), jnp.float32)

    first = mat[:BLOCK, :BLOCK]
    own = jnp.concatenate(factor_block(lambda g: first[8 * g:8 * g + 8, :], lane, row), axis=0)
    for k in range(BLOCKS):
        at = k * BLOCK
        after = at + BLOCK
        here = slice(at, after)
        mat[here, here] = own
        high, low = split(own)
        left = jnp.concatenate([high, low], axis=1)
        for start, stop in ((0, at), (after, NB)):
            if start < stop:
                up, down = split(mat[here, start:stop])
                mat[here, start:stop] = dot(left, jnp.concatenate([up, up], axis=0)) + dot(high, down)
        inverse = jnp.concatenate(
            [
                mat[at + 64 * to_z + 16 * to_y + 8 * to_core:at + 64 * to_z + 16 * to_y + 8 * to_core + 8, :after]
                for to_core in range(CORES)
                for to_z in range(2)
                for to_y in range(Y)
            ],
            axis=0,
        ).astype(jnp.bfloat16)
        local = dot(inverse, products[:after, :]).astype(jnp.bfloat16)
        for to_core in range(CORES):
            for to_z in range(2):
                begin = 64 * to_core + 32 * to_z
                ready[k, to_core, to_z] = local[begin:begin + 32, :]
        leave.pair(k).start()
        leave.start(0, k)
        if k:
            leave.start(1, k - 1)
        if after < NB:
            turned_high, turned_low = split(mat[here, after:].T)
            turned = jnp.concatenate([turned_high, turned_low], axis=1)

            def change(begin, end, start, stop):
                rows = slice(begin - after, end - after)
                up, down = split(mat[here, start:stop])
                return dot(turned[rows], jnp.concatenate([up, up], axis=0)) + dot(turned_high[rows], down)

            following = slice(after, after + BLOCK)
            corner = mat[following, following] - change(after, after + BLOCK, after, after + BLOCK)
            own = jnp.concatenate(factor_block(lambda g: corner[8 * g:8 * g + 8, :], lane, row), axis=0)
            mat[after:, here] = -change(after, NB, at, after)
            for start in range(0, at, 256):
                stop = min(start + 256, at)
                mat[after:, start:stop] = mat[after:, start:stop] - change(after, NB, start, stop)
            for start in range(after, NB, 256):
                stop = min(start + 256, NB)
                mat[after:stop, start:stop] = mat[after:stop, start:stop] - change(after, stop, start, stop)
    leave.start(1, BLOCKS - 1)


def whole_kernel(orbitals, piece, out, *scratch):
    buffers, sems = scratch[:BUFFERS], scratch[BUFFERS:]
    (
        beside, landed, slab, rows, across, products, gram, theirs, terms, mat, ready, beside2, landed2, ordered,
    ) = buffers[:14]
    spot = place()
    greet(*spot, True)
    gather_part(orbitals, piece, slab, rows, across, beside, landed, sems[:7], sems[7:11], spot)
    gram_part(across, slab, products, gram, theirs, terms, buffers[14:], sems[11:21], spot)
    leave = Leave(ready, beside2, landed2, sems[21:26], spot)
    solve(gram, products, mat, leave)
    plane_part(landed2, ordered, out, leave.arrive, sems[26:29], spot)
    leave.finish()


BUFFERS = 26


def whole(orbitals, piece):
    points = orbitals.shape[-1]
    dma = pltpu.SemaphoreType.DMA
    narrow, wide = jnp.bfloat16, jnp.float32
    entries = (Z, Y, CORES, X, 2, points)
    held = Y * X * 2
    buffers = [
        pltpu.VMEM((Z, Y, X, 2, points), narrow),
        pltpu.VMEM((CORES, Z, Y, X, 2, points), narrow),
        pltpu.VMEM(entries, narrow),
        pltpu.VMEM((Z, Y, CORES, X, 16, 128), narrow),
        pltpu.VMEM((NB, NB), narrow),
        pltpu.VMEM((NB, points), narrow),
        pltpu.VMEM((TILES, 8, 128), wide),
        pltpu.VMEM((NB, points), narrow),
        pltpu.VMEM((TILES // 2, 8, 128), wide),
        pltpu.VMEM((NB, NB), wide),
        pltpu.VMEM((BLOCKS, CORES, 2, held, points), narrow),
        pltpu.VMEM((BLOCKS, 2, held, points), narrow),
        pltpu.VMEM((Z, CORES, held, points), narrow),
        pltpu.VMEM((Z, CORES, Y, X, 2, points), narrow),
    ]
    for unit in UNITS:
        buffers += [
            pltpu.VMEM((2, 2, 2 * unit, 8, 128), wide),
            pltpu.VMEM((2, 2, 4 * unit, 8, 128), wide),
            pltpu.VMEM((2, 3, unit, 8, 128), wide),
            pltpu.VMEM((Z - 1, 2, 8, 128), wide),
            pltpu.VMEM((unit, 2, 8, 128), wide),
            pltpu.VMEM((unit, 2, 8, 128), wide),
        ]
    sems = [
        dma, dma, dma((2, Z)), dma((2, Z)), dma((2, 4, X * Y)), dma((2, 4, X * Y)), dma((10,)),
        dma((Z,)), dma((Z,)), dma((3, 4)), dma((3, 4)),
        dma((2, 3, 2, 4)), dma((2, 3, 2, 4)), dma((2, 3, 2, 4)), dma((2, 3, 2, 4)),
        dma((2, Z)), dma((2, Z)), dma((2, Z)), dma((2, Z)), dma((4,)), dma((4,)),
        dma((BLOCKS,)), dma((BLOCKS,)), dma((2, Z)), dma((2, Z)), dma((2,)),
        dma((4, X * Y)), dma((4, X * Y)), dma((4,)),
    ]
    return pl.pallas_call(
        whole_kernel,
        out_shape=jax.ShapeDtypeStruct(entries, narrow),
        in_specs=[pl.BlockSpec(memory_space=pltpu.VMEM)] * 2,
        out_specs=pl.BlockSpec(memory_space=pltpu.VMEM),
        scratch_shapes=buffers + sems,
        compiler_params=pltpu.CompilerParams(collective_id=0, has_side_effects=True, vmem_limit_bytes=VMEM),
        name="localize",
    )(orbitals, piece)


def pick(orbitals, pivots):
    folded = orbitals.reshape(2, 1024, 128)
    outer = (pivots[:, None] // 128 == jnp.arange(1024, dtype=jnp.int32)[None, :]).astype(jnp.bfloat16)
    inner = pivots[:, None] % 128 == jnp.arange(128, dtype=jnp.int32)[None, :]
    rows = jnp.einsum("jh,rhl->rjl", outer, folded, preferred_element_type=jnp.float32)
    return jnp.sum(jnp.where(inner[None], rows, 0.0), axis=2).astype(jnp.bfloat16)


def body(orbitals, pivots):
    points = orbitals.shape[1] // 512
    entries = (Z, Y, CORES, X, 2, points)
    piece = pick(orbitals, pivots).reshape(16, 128)
    outgoing = orbitals.reshape(2, 512, points).transpose(1, 0, 2).reshape(entries)
    returned = whole(outgoing, piece)
    return returned.reshape(512, 2, points).transpose(1, 0, 2).reshape(orbitals.shape)


def solution(mesh):
    placed = (P(("grid", "band"), None), P())
    return jax.shard_map(
        body, mesh=mesh, in_specs=placed, out_specs=P(("grid", "band"), None), check_vma=False
    )
```

```python
import functools
import math

import jax
import jax.numpy as jnp
from jax import lax
from jax.experimental import pallas as pl
from jax.experimental.pallas import tpu as pltpu
from jax.sharding import PartitionSpec as P

MESH = pl.DeviceIdType.MESH
X, Y, Z, CORES = 4, 4, 16, 2
NB = 1024
BLOCK = 128
BLOCKS = NB // BLOCK
TILES = 576
UNITS = (5, 4)
OWNERS = (0, 8)
ROWS_OF_CORE = ((0, 3, 4, 7), (1, 2, 5, 6))
VMEM = 48 * 1024 * 1024


def place():
    grid = lax.axis_index("grid")
    return lax.axis_index("band"), lax.rem(grid // CORES, Y), grid // (CORES * Y), lax.rem(grid, CORES)


def device(x, y, z, core):
    return ((z * Y + y) * CORES + core, x)


def greet(x, y, z, core, plane):
    barrier = pltpu.get_barrier_semaphore()
    partners = [device(x, y, z, 1 - core)]
    for along_y in range(Y):
        for along_x in range(X):
            if (along_x or along_y) and (plane or not (along_x and along_y)):
                partners.append(device(lax.rem(x + along_x, X), lax.rem(y + along_y, Y), z, core))
    for step in range(1, Z):
        partners.append(device(x, y, lax.rem(z + step, Z), core))
    for partner in partners:
        pl.semaphore_signal(barrier, inc=1, device_id=partner, device_id_type=MESH)
    pl.semaphore_wait(barrier, len(partners))


def remote(src, dst, send, recv, target):
    return pltpu.make_async_remote_copy(
        src_ref=src, dst_ref=dst, send_sem=send, recv_sem=recv, device_id=target, device_id_type=MESH
    )


def order_of_z():
    steps = []
    for step in range(1, Z // 2 + 1):
        steps.append(step)
        if step != Z - step:
            steps.append(Z - step)
    return steps


class Regroup:
    def __init__(self, source, out, beside, landed, sems, spot):
        self.source, self.out, self.beside, self.landed = source, out, beside, landed
        self.p_send, self.p_recv, self.z_send, self.z_recv, self.y_send, self.y_recv, self.local = sems
        self.x, self.y, self.z, self.core = spot
        self.origin = (self.core, 1 - self.core)
        self.pair = remote(
            source.at[:, :, 1 - self.core], beside, self.p_send, self.p_recv,
            device(self.x, self.y, self.z, 1 - self.core),
        )
        self.done = []
        self.plane = []
        self.kept = []

    def leaving(self, path, z):
        return self.source.at[z, :, self.core] if path == 0 else self.beside.at[z]

    def landing(self, path, z):
        return self.landed.at[self.origin[path], z]

    def start_z(self, path):
        x, y, z, core = self.x, self.y, self.z, self.core
        if path == 1:
            self.pair.wait_recv()
        for step in order_of_z():
            target = lax.rem(z + step, Z)
            copy = remote(
                self.leaving(path, target), self.landing(path, z), self.z_send.at[path, step], self.z_recv.at[path, z],
                device(x, y, target, core),
            )
            copy.start()
            self.done.append(copy)
        pltpu.make_async_copy(self.leaving(path, z), self.landing(path, z), self.local.at[path]).start()

    def arrive(self, path, source):
        spot = self.landing(path, source)

        @pl.when(self.z != source)
        def _():
            remote(
                spot, spot, self.z_send.at[path, 0], self.z_recv.at[path, source],
                device(self.x, self.y, source, self.core),
            ).wait_recv()

        @pl.when(self.z == source)
        def _():
            pltpu.make_async_copy(spot, spot, self.local.at[path]).wait()

    def start_plane(self, path):
        x, y, z, core = self.x, self.y, self.z, self.core
        origin = self.origin[path]
        for turn, offset in enumerate((0, 1, 3, 2)):
            first = lax.rem(z // 4 + offset, 4) * 4
            for step in range(4):
                self.arrive(path, first + step)
            group = pl.ds(first, 4)
            landing = self.out.at[group, y, origin, x]
            for along_y in range(Y):
                for along_x in range(X):
                    if along_x or along_y:
                        to_x, to_y = lax.rem(x + along_x, X), lax.rem(y + along_y, Y)
                        index = along_y * X + along_x
                        copy = remote(
                            self.landed.at[origin, group, to_y, to_x], landing,
                            self.y_send.at[path, turn, index], self.y_recv.at[path, turn, index],
                            device(to_x, to_y, z, core),
                        )
                        copy.start()
                        self.plane.append(copy)
            keep = pltpu.make_async_copy(
                self.landed.at[origin, group, y, x], landing, self.local.at[2 + 4 * path + turn]
            )
            keep.start()
            self.kept.append(keep)

    def finish(self):
        for copy in self.plane:
            copy.wait_recv()
        for keep in self.kept:
            keep.wait()
        for copy in self.plane + self.done + [self.pair]:
            copy.wait_send()


def pick_part(orbitals, pivots, folded, chosen, piece):
    points = orbitals.shape[-1]
    for part in range(BLOCKS):
        folded[part * BLOCK:(part + 1) * BLOCK, :] = orbitals[2 * part:2 * part + 2].reshape(BLOCK, points)
    outer = pivots[...] // points
    inner = pivots[...] - outer * points
    lines = []
    for orbital in range(2):
        for part in range(BLOCKS):
            index = lax.broadcasted_iota(jnp.int32, (BLOCK, NB), 0) + part * BLOCK
            chosen[part * BLOCK:(part + 1) * BLOCK, :] = jnp.where(
                index == 2 * outer + orbital, 1.0, 0.0
            ).astype(jnp.bfloat16)
        for start in range(0, NB, 256):
            values = lax.dot_general(
                folded[...], chosen[:, start:start + 256], (((0,), (0,)), ((), ())), preferred_element_type=jnp.float32
            )
            here = lax.broadcasted_iota(jnp.int32, values.shape, 0) == inner[:, start:start + 256]
            line = jnp.sum(jnp.where(here, values, 0.0), axis=0, keepdims=True)
            lines += [line[:, :128], line[:, 128:]]
    piece[...] = jnp.concatenate(lines, axis=0).astype(jnp.bfloat16)


def gather_part(orbitals, pivots, piece, slab, rows, across, folded, beside, landed, moving, sems, spot):
    q_send, q_recv, send, recv = sems
    x, y, z, core = spot
    regroup = Regroup(orbitals, slab, beside, landed, moving, (x, y, z, core))
    regroup.pair.start()
    regroup.start_z(0)
    pick_part(orbitals, pivots, folded, across, piece)
    first = []
    for step in order_of_z():
        copy = remote(
            piece, rows.at[z, y, core, x], q_send.at[step], q_recv.at[step], device(x, y, lax.rem(z + step, Z), core)
        )
        copy.start()
        first.append(copy)
    regroup.start_z(1)
    rows[z, y, core, x] = piece[...]
    for copy in first:
        copy.wait_recv()
    second = []
    mine = rows.at[:, y, core, x]
    for step in range(1, Y):
        copy = remote(
            mine, mine, send.at[0, step], recv.at[0, step], device(x, lax.rem(y + step, Y), z, core)
        )
        copy.start()
        second.append(copy)
    for copy in second:
        copy.wait_recv()
    sibling = device(x, y, z, 1 - core)
    near, far, last = [], [], []

    def along_x(step):
        return device(lax.rem(x + step, X), y, z, core)

    def forward(index, ref):
        copy = remote(ref, ref, send.at[2, index], recv.at[2, index], sibling)
        copy.start()
        last.append(copy)

    mine = rows.at[:, :, core, x]
    for index, step in ((0, 1), (1, 3)):
        copy = remote(mine, mine, send.at[1, index], recv.at[1, index], along_x(step))
        copy.start()
        near.append(copy)
    forward(0, mine)
    for index, step in ((0, 1), (1, 3)):
        near[index].wait_recv()
        source = lax.rem(x + 4 - step, X)
        ref = rows.at[pl.ds(index * (Z // 2), Z // 2), :, core, source]
        copy = remote(ref, ref, send.at[1, 2 + index], recv.at[1, 2 + index], along_x(step))
        copy.start()
        far.append(copy)
        forward(1 + index, rows.at[:, :, core, source])
    regroup.start_plane(0)
    for copy in far:
        copy.wait_recv()
    forward(3, rows.at[:, :, core, lax.rem(x + 2, X)])
    for copy in last:
        copy.wait_recv()
    for part in range(BLOCKS):
        block = rows[2 * part:2 * part + 2].reshape(64, 16, 128).reshape(128, 8, 128).reshape(128, NB)
        across[:, part * BLOCK:(part + 1) * BLOCK] = block.T
    regroup.start_plane(1)
    regroup.finish()
    for copy in first + second + near + far + last:
        copy.wait_send()


def plane_part(landed, ordered, out, arrive, sems, spot):
    send, recv, kept = sems
    x, y, z, core = spot
    copies = []
    keeps = []
    for turn, offset in enumerate((0, 1, 3, 2)):
        first = lax.rem(z // 4 + offset, 4) * 4
        for step in range(4):
            arrive(first + step)
        group = pl.ds(first, 4)
        ordered[group] = landed[group].reshape(4, CORES, Y, X, 2, landed.shape[-1])
        landing = out.at[group, y, :, x]
        for along_y in range(Y):
            for along_x in range(X):
                if along_x or along_y:
                    to_x, to_y = lax.rem(x + along_x, X), lax.rem(y + along_y, Y)
                    index = along_y * X + along_x
                    copy = remote(
                        ordered.at[group, :, to_y, to_x], landing, send.at[turn, index], recv.at[turn, index],
                        device(to_x, to_y, z, core),
                    )
                    copy.start()
                    copies.append(copy)
        keep = pltpu.make_async_copy(ordered.at[group, :, y, x], landing, kept.at[turn])
        keep.start()
        keeps.append(keep)
    for copy in copies:
        copy.wait_recv()
    for copy in copies:
        copy.wait_send()
    for keep in keeps:
        keep.wait()


def sum_wave(wave, out, terms, buffers, sems, spot):
    got0, got1, got2, got3, plane, summed = buffers
    send, recv, r_send, r_recv, z_send, z_recv, g_send, g_recv = sems
    x, y, z, core = spot
    unit = UNITS[wave]
    first_owner = OWNERS[wave]
    half = 16 * unit
    block = 4 * unit
    middle = block // 2
    begin = sum(UNITS[:wave]) * 32
    goal = core * (TILES // 2) + begin
    firsts = (x, y)
    seconds = (y, x)
    sent = []

    def mate(axis_is_x, step):
        if axis_is_x:
            return device(lax.rem(x + step, X), y, z, core)
        return device(x, lax.rem(y + step, Y), z, core)

    def span(base, h, where, start=0, size=block):
        return pl.ds(base + h * half + lax.rem(firsts[h] + where, 4) * block + start, size)

    def launch(*args):
        copy = remote(*args)
        copy.start()
        sent.append(copy)
        return copy

    far = [
        (h, index, step, launch(
            terms.at[span(begin, h, 2, index * middle, middle)], got0.at[h, index],
            r_send.at[wave, 0, h, index], r_recv.at[wave, 0, h, index], mate(h == 0, step),
        ))
        for h in range(2) for index, step in ((0, 1), (1, 3))
    ]
    yield
    near = []
    for h, index, step, copy in far:
        copy.wait_recv()
        part = span(begin, h, step, index * middle, middle)
        terms[part] = terms[part] + got0[h, index]
        near.append(launch(
            terms.at[span(begin, h, step)], got1.at[h, index], r_send.at[wave, 2, h, index],
            r_recv.at[wave, 2, h, index], mate(h == 0, step),
        ))
    yield
    for copy in near:
        copy.wait_recv()
    later = []
    for h in range(2):
        mine = span(begin, h, 0)
        terms[mine] = terms[mine] + (got1[h, 0] + got1[h, 1])
    for step in range(1, 4):
        for h in range(2):
            target = lax.rem(seconds[h] + step, 4)
            later.append(launch(
                terms.at[pl.ds(begin + h * half + (firsts[h] * 4 + target) * unit, unit)], got2.at[h, step - 1],
                r_send.at[wave, 1, h, step], r_recv.at[wave, 1, h, step], mate(h == 1, step),
            ))
    yield
    for copy in later:
        copy.wait_recv()
    starts = [h * half + (firsts[h] * 4 + seconds[h]) * unit for h in range(2)]
    for h in range(2):
        mine = pl.ds(begin + starts[h], unit)
        plane[:, h] = terms[mine] + (got2[h, 0] + got2[h, 1]) + got2[h, 2]

    def owns(where):
        return (where >= first_owner) & (where < first_owner + unit)

    def tile_of(where):
        return jnp.clip(where - first_owner, 0, unit - 1)

    def to_owner(step):
        target = lax.rem(z + step, Z)
        return target, remote(
            plane.at[tile_of(target)], got3.at[step - 1], z_send.at[wave, step], z_recv.at[wave, step],
            device(x, y, target, core),
        )

    for step in order_of_z():
        target, copy = to_owner(step)

        @pl.when(owns(target))
        def _():
            copy.start()

    yield
    tile = tile_of(z)

    def to_all(step, which):
        return remote(
            summed.at[which], summed.at[which], g_send.at[wave, step], g_recv.at[wave, step],
            device(x, y, lax.rem(z + step, Z), core),
        )

    @pl.when(owns(z))
    def _():
        for step in order_of_z():
            to_owner(step)[1].wait_recv()
        total = plane[tile]
        for step in range(1, Z):
            total = total + got3[step - 1]
        summed[tile] = total
        for step in order_of_z():
            to_all(step, tile).start()

    yield
    for step in order_of_z():
        source = lax.rem(z + Z - step, Z)

        @pl.when(owns(source))
        def _():
            to_all(step, tile_of(source)).wait_recv()

    inner = []
    for h in range(2):
        own = pl.ds(goal + starts[h], unit)
        out[own] = summed[:, h]
        for step in range(1, 4):
            inner.append(launch(
                out.at[own], out.at[own], send.at[wave, 0, h, step], recv.at[wave, 0, h, step], mate(h == 1, step)
            ))
    yield
    for copy in inner:
        copy.wait_recv()
    across = []

    def forward(h, index, ref):
        across.append(launch(
            ref, ref, send.at[wave, 2, h, index], recv.at[wave, 2, h, index], device(x, y, z, 1 - core)
        ))

    near = []
    for h in range(2):
        ref = out.at[span(goal, h, 0)]
        for index, step in ((0, 1), (1, 3)):
            near.append((h, index, step, launch(
                ref, ref, send.at[wave, 1, h, index], recv.at[wave, 1, h, index], mate(h == 0, step)
            )))
    for h in range(2):
        forward(h, 0, out.at[span(goal, h, 0)])
    yield
    far = []
    for h, index, step, copy in near:
        copy.wait_recv()
        ref = out.at[span(goal, h, 4 - step, index * middle, middle)]
        far.append(launch(
            ref, ref, send.at[wave, 1, h, 2 + index], recv.at[wave, 1, h, 2 + index], mate(h == 0, step)
        ))
        forward(h, 1 + index, out.at[span(goal, h, 4 - step)])
    yield
    for copy in far:
        copy.wait_recv()
    for h in range(2):
        forward(h, 3, out.at[span(goal, h, 2)])
    yield
    for copy in across:
        copy.wait_recv()
    yield
    for copy in sent:
        copy.wait_send()
    for step in range(1, Z):
        target, copy = to_owner(step)

        @pl.when(owns(target))
        def _():
            copy.wait_send()

    @pl.when(owns(z))
    def _():
        for step in range(1, Z):
            to_all(step, tile).wait_send()


def gram_part(across, slab, products, out, theirs, terms, buffers, sems, spot):
    p_send, p_recv = sems[-2:]
    x, y, z, core = spot
    pairs = []
    columns = slab[...].reshape(NB, slab.shape[-1])
    for part in range(4):
        rows = slice(part * 256, (part + 1) * 256)
        products[rows, :] = (dot(across[rows, :], columns) * (1.0 / math.sqrt(NB))).astype(jnp.bfloat16)
        pair = remote(
            products.at[rows, :], theirs.at[rows, :], p_send.at[part], p_recv.at[part], device(x, y, z, 1 - core)
        )
        pair.start()
        pairs.append(pair)
    contract = (((1,), (1,)), ((), ()))

    def add(source, again, begin, end):
        for which in range(CORES):

            @pl.when(core == which)
            def _():
                count = sum(BLOCKS - i for i in ROWS_OF_CORE[which][:begin])
                for i in ROWS_OF_CORE[which][begin:end]:
                    row = lax.dot_general(
                        source[i * BLOCK:(i + 1) * BLOCK, :], source[i * BLOCK:, :], contract,
                        preferred_element_type=jnp.float32,
                    )
                    for j in range(BLOCKS - i):
                        tiles = slice(count * 16, (count + 1) * 16)
                        term = row[:, j * BLOCK:(j + 1) * BLOCK].reshape(16, 8, 128)
                        terms[tiles] = terms[tiles] + term if again else term
                        count += 1

    add(products, False, 0, 4)
    for pair in pairs:
        pair.wait_recv()
    add(theirs, True, 0, 2)
    waves = [sum_wave(wave, out, terms, buffers[6 * wave:6 * wave + 6], sems[:-2], spot) for wave in range(2)]
    next(waves[0])
    add(theirs, True, 2, 4)
    next(waves[1])
    while waves:
        waves = [wave for wave in waves if next(wave, waves) is None]
    for pair in pairs:
        pair.wait_send()


def split(value):
    high = value.astype(jnp.bfloat16)
    return high, (value - high.astype(jnp.float32)).astype(jnp.bfloat16)


def dot(a, b):
    return jnp.dot(a, b, preferred_element_type=jnp.float32)


def factor_block(load, lane, row):
    full = (8, 128)
    groups = [load(g) for g in range(16)]
    for quarter in range(4):
        first = 4 * quarter
        for g in range(first, first + 4):
            at = 8 * g
            panel = groups[g]
            columns = [jnp.broadcast_to(panel[:, at + t:at + t + 1], full) for t in range(8)]
            a = [[jnp.broadcast_to(columns[t][i:i + 1, :], full) for t in range(i + 1)] for i in range(8)]
            below = [[None] * 8 for _ in range(8)]
            scale = []
            for s in range(8):
                r = lax.rsqrt(a[s][s])
                scale.append(r)
                for i in range(s + 1, 8):
                    below[i][s] = a[i][s] * r
                for i in range(s + 1, 8):
                    for t in range(s + 1, i + 1):
                        a[i][t] = a[i][t] - below[i][s] * below[t][s]
            inside = (lane >= at) & (lane < at + 8)
            panel = jnp.where(inside, (lane == row + at).astype(jnp.float32), panel)
            solved = []
            for s in range(8):
                value = jnp.broadcast_to(panel[s:s + 1, :], full)
                for t in range(s):
                    value = value - below[s][t] * solved[t]
                solved.append(value * scale[s])
            result = solved[0]
            for s in range(1, 8):
                result = jnp.where(row == s, solved[s], result)
            groups[g] = result
            for other in range(g + 1, first + 4):
                target = groups[other]
                left = []
                for s in range(8):
                    value = jnp.broadcast_to(target[:, at + s:at + s + 1], full)
                    for t in range(s):
                        value = value - below[s][t] * left[t]
                    left.append(value * scale[s])
                target = jnp.where(inside, 0.0, target)
                for s in range(8):
                    target = target - left[s] * solved[s]
                groups[other] = target
        if quarter < 3:
            at = 32 * quarter
            inside = (lane >= at) & (lane < at + 32)
            rows = jnp.concatenate(
                [
                    jnp.where(inside & (lane > 8 * g + row), 0.0, groups[g])
                    for g in range(first, first + 4)
                ],
                axis=0,
            )
            turned = rows.T[at + 32:, :]
            high, low = split(rows)
            turned_high, turned_low = split(turned)
            change = dot(turned_high, high) + dot(turned_low, high) + dot(turned_high, low)
            for other in range(first + 4, 16):
                begin = (other - first - 4) * 8
                groups[other] = jnp.where(inside, 0.0, groups[other]) - change[begin:begin + 8, :]
    return [jnp.where(lane > 8 * g + row, 0.0, groups[g]) for g in range(16)]


class Leave:
    def __init__(self, ready, beside, landed, sems, spot):
        self.ready, self.beside, self.landed = ready, beside, landed
        self.p_send, self.p_recv, self.z_send, self.z_recv, self.local = sems
        self.x, self.y, self.z, self.core = spot

    def pair(self, k):
        return remote(
            self.ready.at[k, 1 - self.core], self.beside.at[k], self.p_send.at[k], self.p_recv.at[k],
            device(self.x, self.y, self.z, 1 - self.core),
        )

    def source(self, path, k, part):
        return self.ready.at[k, self.core, part] if path == 0 else self.beside.at[k, part]

    def origin(self, path):
        return self.core if path == 0 else 1 - self.core

    def along(self, path, k, part):
        return remote(
            self.source(path, k, part), self.landed.at[self.z, self.origin(path)],
            self.z_send.at[path, 2 * k + part], self.z_recv.at[path, self.z],
            device(self.x, self.y, 2 * k + part, self.core),
        )

    def keep(self, path, k, part):
        return pltpu.make_async_copy(
            self.source(path, k, part), self.landed.at[self.z, self.origin(path)], self.local.at[path]
        )

    def start(self, path, k):
        if path == 1:
            self.pair(k).wait_recv()
        for part in range(2):

            @pl.when(self.z != 2 * k + part)
            def _():
                self.along(path, k, part).start()

            @pl.when(self.z == 2 * k + part)
            def _():
                self.keep(path, k, part).start()

    def arrive(self, source):
        @pl.when(self.z != source)
        def _():
            for path in range(2):
                spot = self.landed.at[source, self.origin(path)]
                remote(
                    spot, spot, self.z_send.at[path, source], self.z_recv.at[path, source],
                    device(self.x, self.y, source, self.core),
                ).wait_recv()

        @pl.when(self.z == source)
        def _():
            for path in range(2):
                spot = self.landed.at[source, self.origin(path)]
                pltpu.make_async_copy(spot, spot, self.local.at[path]).wait()

    def finish(self):
        for path in range(2):
            for k in range(BLOCKS):
                for part in range(2):

                    @pl.when(self.z != 2 * k + part)
                    def _():
                        self.along(path, k, part).wait_send()

        for k in range(BLOCKS):
            self.pair(k).wait_send()


def solve(gram, products, mat, leave):
    ready = leave.ready
    lane = lax.broadcasted_iota(jnp.int32, (8, 128), 1)
    row = lax.broadcasted_iota(jnp.int32, (8, 128), 0)
    count = 0
    for rows in ROWS_OF_CORE:
        for i in rows:
            for j in range(i, BLOCKS):
                mat[i * BLOCK:(i + 1) * BLOCK, j * BLOCK:(j + 1) * BLOCK] = (
                    gram[count * 16:(count + 1) * 16].reshape(BLOCK, BLOCK) * (1.0 / 131072.0)
                )
                count += 1
            if i:
                mat[i * BLOCK:(i + 1) * BLOCK, :i * BLOCK] = jnp.zeros((BLOCK, i * BLOCK), jnp.float32)

    first = mat[:BLOCK, :BLOCK]
    own = jnp.concatenate(factor_block(lambda g: first[8 * g:8 * g + 8, :], lane, row), axis=0)
    for k in range(BLOCKS):
        at = k * BLOCK
        after = at + BLOCK
        here = slice(at, after)
        mat[here, here] = own
        high, low = split(own)
        left = jnp.concatenate([high, low], axis=1)
        for start, stop in ((0, at), (after, NB)):
            if start < stop:
                up, down = split(mat[here, start:stop])
                mat[here, start:stop] = dot(left, jnp.concatenate([up, up], axis=0)) + dot(high, down)
        inverse = jnp.concatenate(
            [
                mat[at + 64 * to_z + 16 * to_y + 8 * to_core:at + 64 * to_z + 16 * to_y + 8 * to_core + 8, :after]
                for to_core in range(CORES)
                for to_z in range(2)
                for to_y in range(Y)
            ],
            axis=0,
        ).astype(jnp.bfloat16)
        local = dot(inverse, products[:after, :]).astype(jnp.bfloat16)
        for to_core in range(CORES):
            for to_z in range(2):
                begin = 64 * to_core + 32 * to_z
                ready[k, to_core, to_z] = local[begin:begin + 32, :]
        leave.pair(k).start()
        leave.start(0, k)
        if k:
            leave.start(1, k - 1)
        if after < NB:
            turned_high, turned_low = split(mat[here, after:].T)
            turned = jnp.concatenate([turned_high, turned_low], axis=1)

            def change(begin, end, start, stop):
                rows = slice(begin - after, end - after)
                up, down = split(mat[here, start:stop])
                return dot(turned[rows], jnp.concatenate([up, up], axis=0)) + dot(turned_high[rows], down)

            following = slice(after, after + BLOCK)
            corner = mat[following, following] - change(after, after + BLOCK, after, after + BLOCK)
            own = jnp.concatenate(factor_block(lambda g: corner[8 * g:8 * g + 8, :], lane, row), axis=0)
            mat[after:, here] = -change(after, NB, at, after)
            for start in range(0, at, 256):
                stop = min(start + 256, at)
                mat[after:, start:stop] = mat[after:, start:stop] - change(after, NB, start, stop)
            for start in range(after, NB, 256):
                stop = min(start + 256, NB)
                mat[after:stop, start:stop] = mat[after:stop, start:stop] - change(after, stop, start, stop)
    leave.start(1, BLOCKS - 1)


def whole_kernel(orbitals, pivots, out, *scratch):
    buffers, sems = scratch[:BUFFERS], scratch[BUFFERS:]
    (
        beside, landed, slab, rows, across, products, gram, theirs, terms, mat, ready, beside2, landed2, ordered,
        piece,
    ) = buffers[:15]
    spot = place()
    greet(*spot, True)
    gather_part(orbitals, pivots, piece, slab, rows, across, products, beside, landed, sems[:7], sems[7:11], spot)
    gram_part(across, slab, products, gram, theirs, terms, buffers[15:], sems[11:21], spot)
    leave = Leave(ready, beside2, landed2, sems[21:26], spot)
    solve(gram, products, mat, leave)
    plane_part(landed2, ordered, out, leave.arrive, sems[26:29], spot)
    leave.finish()


BUFFERS = 27


def whole(orbitals, pivots):
    points = orbitals.shape[-1]
    dma = pltpu.SemaphoreType.DMA
    narrow, wide = jnp.bfloat16, jnp.float32
    entries = (Z, Y, CORES, X, 2, points)
    held = Y * X * 2
    buffers = [
        pltpu.VMEM((Z, Y, X, 2, points), narrow),
        pltpu.VMEM((CORES, Z, Y, X, 2, points), narrow),
        pltpu.VMEM(entries, narrow),
        pltpu.VMEM((Z, Y, CORES, X, 16, 128), narrow),
        pltpu.VMEM((NB, NB), narrow),
        pltpu.VMEM((NB, points), narrow),
        pltpu.VMEM((TILES, 8, 128), wide),
        pltpu.VMEM((NB, points), narrow),
        pltpu.VMEM((TILES // 2, 8, 128), wide),
        pltpu.VMEM((NB, NB), wide),
        pltpu.VMEM((BLOCKS, CORES, 2, held, points), narrow),
        pltpu.VMEM((BLOCKS, 2, held, points), narrow),
        pltpu.VMEM((Z, CORES, held, points), narrow),
        pltpu.VMEM((Z, CORES, Y, X, 2, points), narrow),
        pltpu.VMEM((16, 128), narrow),
    ]
    for unit in UNITS:
        buffers += [
            pltpu.VMEM((2, 2, 2 * unit, 8, 128), wide),
            pltpu.VMEM((2, 2, 4 * unit, 8, 128), wide),
            pltpu.VMEM((2, 3, unit, 8, 128), wide),
            pltpu.VMEM((Z - 1, 2, 8, 128), wide),
            pltpu.VMEM((unit, 2, 8, 128), wide),
            pltpu.VMEM((unit, 2, 8, 128), wide),
        ]
    sems = [
        dma, dma, dma((2, Z)), dma((2, Z)), dma((2, 4, X * Y)), dma((2, 4, X * Y)), dma((10,)),
        dma((Z,)), dma((Z,)), dma((3, 4)), dma((3, 4)),
        dma((2, 3, 2, 4)), dma((2, 3, 2, 4)), dma((2, 3, 2, 4)), dma((2, 3, 2, 4)),
        dma((2, Z)), dma((2, Z)), dma((2, Z)), dma((2, Z)), dma((4,)), dma((4,)),
        dma((BLOCKS,)), dma((BLOCKS,)), dma((2, Z)), dma((2, Z)), dma((2,)),
        dma((4, X * Y)), dma((4, X * Y)), dma((4,)),
    ]
    return pl.pallas_call(
        whole_kernel,
        out_shape=jax.ShapeDtypeStruct(entries, narrow),
        in_specs=[pl.BlockSpec(memory_space=pltpu.VMEM)] * 2,
        out_specs=pl.BlockSpec(memory_space=pltpu.VMEM),
        scratch_shapes=buffers + sems,
        compiler_params=pltpu.CompilerParams(collective_id=0, has_side_effects=True, vmem_limit_bytes=VMEM),
        name="localize",
    )(orbitals, pivots)


def body(orbitals, pivots):
    points = orbitals.shape[1] // 512
    entries = (Z, Y, CORES, X, 2, points)
    outgoing = orbitals.reshape(2, 512, points).transpose(1, 0, 2).reshape(entries)
    returned = whole(outgoing, pivots.reshape(1, NB))
    return returned.reshape(512, 2, points).transpose(1, 0, 2).reshape(orbitals.shape)


def solution(mesh):
    placed = (P(("grid", "band"), None), P())
    return jax.shard_map(
        body, mesh=mesh, in_specs=placed, out_specs=P(("grid", "band"), None), check_vma=False
    )
```
